512 devices in a mesh: dp: 128 (over z, x, core), mp: 4 (over y).
Axes of the slice: x: 4, y: 4, z: 16, core: 2. Of those that a mesh axis runs over, the one named last changes fastest.
Arguments:
- queries: bfloat16 [114688, 2048], P('dp', 'mp'), may hold values from -20 to 20
- out_grad: bfloat16 [114688, 2048], P('dp', 'mp'), may hold values from -6 to 6
- store: bfloat16 [2048, 64, 512], P('dp', None, 'mp'), may hold values from -7 to 7
- key_weight: bfloat16 [512, 2048], P('dp', 'mp'), may hold values from -1 to 1
- value_weight: bfloat16 [512, 2048], P('dp', 'mp'), may hold values from -0.25 to 0.25
- owner: int32 [1792, 2], P('dp'), may hold values from 0 to 127, all different within a row; in each aligned block of 14 rows (0 to 13, 14 to 27, ...) no two rows name the same one
- row: int32 [1792, 2], P('dp'), may hold values from 0 to 15
- valid: int32 [1792, 2], P('dp'), may hold values from 16 to 64
Outputs:
- attended: bfloat16 [114688, 2048], P('dp', 'mp')
- key_grad: float32 [512, 2048], P('dp', 'mp')
- value_grad: float32 [512, 2048], P('dp', 'mp')
The draws below stay inside these ranges and needn't reach their ends.
Inputs may be any that keep to these rules, and one draw needn't show every extreme that they name: Within the 14 query blocks of one index of dp (aligned blocks of rows) no owner is named more than 1 times, a bound that some block reaches; the 2 neighbours of one query block have different owners; every owner is named somewhere.
All inputs are finite; a program needn't handle non-finite values.
Results may differ from the reference program's by a relative error of at most 0.009.
The reference program's roundings to bfloat16 on the way (of `neighbours`, `key_states`, `rounded`, `grad_score`, `key_cot` and `value_cot`) count: a program that leaves them out, or rounds other values in their place, can miss the bound.
Values may be sent and summed in bfloat16 or wider, within the bound.
A program may use at most 64 MiB of HBM per device.

```python
import math
import jax
import jax.numpy as jnp
import numpy as np
from jax import lax

HEAD_DIM = 128
HEADS = 16
ENC_WIDTH = 512
BLOCK_LEN = 64
NEIGH = 2
NB_LEN = 64
BLOCKS_DEV = 14
STORE_DEV = 16
CAP = 1
TOKENS = 114688
BLOCKS = 1792
STORE_ALL = 2048
N_DP = 128


def draw_queries(key, part):
    key = jax.random.fold_in(key, 1)
    shape = (TOKENS, HEADS * HEAD_DIM)
    values = jnp.clip(jax.random.normal(key, shape, jnp.float32), -6.0, 6.0)
    return values.astype(jnp.bfloat16)


def draw_store(key, part):
    key = jax.random.fold_in(key, 2)
    shape = (STORE_ALL, NB_LEN, ENC_WIDTH)
    values = jnp.clip(jax.random.normal(key, shape, jnp.float32), -6.0, 6.0)
    return values.astype(jnp.bfloat16)


def draw_key_weight(key, part):
    key = jax.random.fold_in(key, 3)
    shape = (ENC_WIDTH, HEADS * HEAD_DIM)
    values = jnp.clip(jax.random.normal(key, shape, jnp.float32), -4.0, 4.0) * ENC_WIDTH ** (-0.5)
    return values.astype(jnp.bfloat16)


def set_ends(values, rng, smallest, top_value):
    place = [jax.random.randint(jax.random.fold_in(rng, axis), (), 0, length) for axis, length in enumerate(values.shape)]
    main_axis = values.shape.index(max(values.shape))
    neighbour = place[:main_axis] + [(place[main_axis] + 1) % values.shape[main_axis]] + place[main_axis + 1:]
    return values.at[tuple(place)].set(smallest).at[tuple(neighbour)].set(top_value)


def level_of(own_key, dims, shards, smallest, top_value):
    gain = 1.0
    for position, parts in shards:
        draws = jax.random.uniform(jax.random.fold_in(jax.random.fold_in(own_key, 6), position), (parts,), jnp.float32, smallest / len(shards), top_value / len(shards))
        gain = gain * jnp.repeat(jnp.exp(draws), dims[position] // parts).reshape((-1,) + (1,) * (len(dims) - 1 - position))
    return gain


def shared_out(own_key, own, number, rows, count, top, limit, lean):
    sequence = jax.random.permutation(own_key, count)
    packed, ordinary = load_shares(count, rows * top, limit, lean, True), load_shares(count, rows * top, limit, lean, False)
    places = jnp.arange(count)

    def named(sizes, rotation):
        used = int((sizes > 0).sum())
        fixed = max(1, used // 4)
        shifted = fixed + (places - fixed + rotation * (used - fixed)) % max(1, count - fixed)
        return jnp.zeros((count,), jnp.int32).at[sequence[jnp.where(places < fixed, places, shifted)]].set(jnp.asarray(sizes, jnp.int32))

    sizes = jnp.where(number % 4 == 0, named(packed, number // 4), named(ordinary, number - number // 4 - 1))
    mixed = jax.random.permutation(jax.random.fold_in(own, 3), count)
    donor, sink = mixed[0:count // 2 * 2:2], mixed[1:count // 2 * 2:2]
    room = jnp.minimum(sizes[donor] - 1, limit - sizes[sink]) // 2
    room = jnp.where((donor == sequence[0]) | (sink == sequence[0]) | (sizes[sink] == 0), 0, jnp.maximum(room, 0))
    shifted = jax.random.randint(jax.random.fold_in(own, 4), (count // 2,), 0, 1 << 20) % (room + 1)
    sizes = sizes.at[donor].add(-shifted).at[sink].add(shifted)
    items = jnp.searchsorted(jnp.cumsum(sizes), jnp.arange(rows * top), side="right").astype(jnp.int32)
    listing = items.reshape(top, rows).T
    listing = listing[jax.random.permutation(jax.random.fold_in(own, 1), rows)]
    rotation = jax.random.randint(jax.random.fold_in(own, 2), (rows, 1), 0, top)
    return jnp.take_along_axis(listing, (jnp.arange(top)[None, :] + rotation) % top, axis=1)


def load_shares(count, total, limit, lean, full):
    loads = [(1 << 20) // math.isqrt(standing ** lean) + 1 for standing in range(1, count + 1)]
    largest = limit if full else min(limit, max(-(-total // count), total * loads[0] // sum(loads)))
    least = 1 if total - largest >= count - 1 else 0
    holding, rest = [largest] + [least] * (count - 1), total - largest - least * (count - 1)
    while rest > 0:
        candidates = [i for i in range(1, count) if holding[i] < largest] or [i for i in range(1, count) if holding[i] < limit]
        whole, budget = sum([loads[i] for i in candidates]), rest
        for i in candidates:
            addition = min(limit - holding[i], max(1, budget * loads[i] // whole), rest)
            holding[i] = holding[i] + addition
            rest = rest - addition
    return np.array(holding)


def normal_values(stream_key, dims, spread, bound, cuts=(), kind=jnp.bfloat16):
    drawn = jax.random.normal(stream_key, dims, jnp.float32) * spread
    if len(cuts) > 0:
        drawn = level_of(stream_key, dims, cuts, -0.22, 0.18) * drawn
    return jnp.clip(drawn, min=-bound, max=bound).astype(kind)


def setup_inputs(seed: int = 0) -> dict:
    splits = jax.random.split(jax.random.key(seed), 9)
    queries = draw_queries(jax.random.fold_in(splits[8], 71), 0)
    out_grad = normal_values(splits[1], (TOKENS, HEADS * HEAD_DIM), 1.0, 6.0, ((0, 128), (1, 4)))
    store = draw_store(jax.random.fold_in(splits[8], 71), 0)
    key_weight = draw_key_weight(jax.random.fold_in(splits[8], 71), 0)
    value_weight = normal_values(splits[4], (ENC_WIDTH, HEADS * HEAD_DIM), ENC_WIDTH ** -0.5, 0.25, ((0, 128), (1, 4)))
    owner_keys = jax.random.split(jax.random.fold_in(splits[5], 1), BLOCKS // BLOCKS_DEV)
    owner_turns = jax.random.permutation(jax.random.fold_in(splits[5], 3), BLOCKS // BLOCKS_DEV)
    owner = jax.vmap(lambda own, number: shared_out(jax.random.fold_in(splits[5], 2), own, number, BLOCKS_DEV, N_DP, NEIGH, CAP, 2))(owner_keys, owner_turns).reshape((BLOCKS, NEIGH))
    row = set_ends(jax.random.randint(splits[6], (BLOCKS, NEIGH), 0, STORE_DEV), jax.random.fold_in(splits[6], 1), 0, STORE_DEV - 1).astype(jnp.int32)
    valid = set_ends(jax.random.randint(splits[7], (BLOCKS, NEIGH), NB_LEN // 4, NB_LEN + 1), jax.random.fold_in(splits[7], 1), NB_LEN // 4, NB_LEN).astype(jnp.int32)
    return {"queries": queries, "out_grad": out_grad, "store": store, "key_weight": key_weight, "value_weight": value_weight, "owner": owner, "row": row, "valid": valid}


def attend_block(query_heads, grad_heads, neighbours, allowed, key_weight, value_weight):
    factor = 1.0 / math.sqrt(HEAD_DIM)
    block_count = query_heads.shape[0]
    head_count = query_heads.shape[2]
    flat_rows = neighbours.reshape(-1, neighbours.shape[-1])
    key_states = jnp.dot(flat_rows, key_weight, preferred_element_type=jnp.float32).astype(jnp.bfloat16)
    value_states = jnp.dot(flat_rows, value_weight, preferred_element_type=jnp.float32).astype(jnp.bfloat16)
    key_heads = key_states.reshape(block_count, -1, head_count, HEAD_DIM).astype(jnp.float32)
    value_heads = value_states.reshape(block_count, -1, head_count, HEAD_DIM).astype(jnp.float32)
    query_wide = query_heads.astype(jnp.float32)
    grad_wide = grad_heads.astype(jnp.float32)
    scores = factor * jnp.einsum('cihd,ckhd->chik', query_wide, key_heads)
    scores = jnp.where(allowed[:, None, None, :], scores, -jnp.inf)
    highest = lax.optimization_barrier(jnp.max(scores, axis=-1, keepdims=True))
    exponent = jnp.exp(scores - highest)
    probability = exponent / lax.optimization_barrier(jnp.sum(exponent, axis=-1, keepdims=True))
    rounded = probability.astype(jnp.bfloat16)
    attended = jnp.einsum('chik,ckhd->cihd', rounded.astype(jnp.float32), value_heads).astype(jnp.bfloat16)
    grad_prob = jnp.einsum('cihd,ckhd->chik', grad_wide, value_heads)
    grad_score = (probability * (grad_prob - lax.optimization_barrier(jnp.sum(probability * grad_prob, axis=-1, keepdims=True)))).astype(jnp.bfloat16)
    key_cot = (factor * jnp.einsum('chik,cihd->ckhd', grad_score.astype(jnp.float32), query_wide)).astype(jnp.bfloat16)
    value_cot = jnp.einsum('chik,cihd->ckhd', rounded.astype(jnp.float32), grad_wide).astype(jnp.bfloat16)
    token_count = flat_rows.shape[0]
    key_part = jnp.dot(flat_rows.T, key_cot.reshape(token_count, -1), preferred_element_type=jnp.float32)
    value_part = jnp.dot(flat_rows.T, value_cot.reshape(token_count, -1), preferred_element_type=jnp.float32)
    return (attended, key_part, value_part)

def reference(queries, out_grad, store, key_weight, value_weight, owner, row, valid):
    head_width = HEADS * HEAD_DIM
    query_all = queries.reshape(N_DP, BLOCKS_DEV, BLOCK_LEN, HEADS, HEAD_DIM)
    grad_all = out_grad.reshape(N_DP, BLOCKS_DEV, BLOCK_LEN, HEADS, HEAD_DIM)
    source_rows = (owner * STORE_DEV + row).astype(jnp.int32).reshape(N_DP, BLOCKS_DEV, NEIGH)
    length_all = valid.reshape(N_DP, BLOCKS_DEV, NEIGH)
    positions = lax.iota(jnp.int32, NB_LEN)

    def step_fn(running, inputs):
        query_heads, grad_heads, sources, lengths = inputs
        neighbours = jnp.take(store, sources.reshape(-1), axis=0)
        allowed = (positions[None, None, :] < lengths[:, :, None]).reshape(BLOCKS_DEV, NEIGH * NB_LEN)
        attended, key_part, value_part = attend_block(query_heads, grad_heads, neighbours, allowed, key_weight, value_weight)
        return ((running[0] + key_part, running[1] + value_part), attended)
    empty_sum = jnp.zeros((ENC_WIDTH, head_width), jnp.float32)
    totals, attended = lax.scan(step_fn, (empty_sum, empty_sum), (query_all, grad_all, source_rows, length_all))
    return (attended.reshape(TOKENS, head_width), totals[0], totals[1])
```

```python
import functools
import math

import jax
import jax.numpy as jnp
from jax import lax
from jax.experimental import pallas as pl
from jax.experimental.pallas import tpu as pltpu
from jax.sharding import PartitionSpec as P

HEAD_DIM = 128
ENC_WIDTH = 512
BLOCK_LEN = 64
NEIGH = 2
NB_LEN = 64
BLOCKS = 14
SLOTS = BLOCKS * NEIGH
ROWS = SLOTS * NB_LEN
HEADS_DEV = 4
WIDTH = HEADS_DEV * HEAD_DIM
NZ, NX, NY, PLANE = 16, 4, 4, 8
CHUNKS = 7
PER = SLOTS // CHUNKS

MESH = pl.DeviceIdType.MESH
F32 = jnp.float32
BF16 = jnp.bfloat16
VM = pltpu.VMEM
VSPEC = pl.BlockSpec(memory_space=pltpu.VMEM)
SSPEC = pl.BlockSpec(memory_space=pltpu.SMEM)
VLIMIT = 56 * 2**20


def remote(src, dst, send, recv, device):
    return pltpu.make_async_remote_copy(
        src_ref=src,
        dst_ref=dst,
        send_sem=send,
        recv_sem=recv,
        device_id=device,
        device_id_type=MESH,
    )


def greet(devices):
    barrier = pltpu.get_barrier_semaphore()
    for device in devices:
        pl.semaphore_signal(barrier, inc=1, device_id=device, device_id_type=MESH)
    pl.semaphore_wait(barrier, len(devices))


def fetch_kernel(
    store, kw, vw, owner_v, row_v, owner_s, nb, wout, *scratch
):
    planes = scratch[:15]
    tab_v, tab_s, stage, got, wall = scratch[15:20]
    sems = scratch[20:]
    ring_s, ring_r, wring_s, wring_r, cell_s, cell_r, wc_s, wc_r = sems[:8]
    tab_ss, tab_rs, tab_ls, ys_s, ys_r, yf_s, yf_r = sems[8:]
    ups = [store] + [planes[2 * s - 2] for s in range(1, 8)] + [planes[14]]
    dns = [store] + [planes[2 * s - 1] for s in range(1, 8)] + [planes[14]]
    me = lax.axis_index("dp")
    y = lax.axis_index("mp")
    z, r = me // PLANE, me % PLANE
    zup = (((z + 1) % NZ) * PLANE + r, y)
    zdn = (((z + NZ - 1) % NZ) * PLANE + r, y)
    peer = [(z * PLANE + (r + t) % PLANE, y) for t in range(PLANE)]
    yup, ydn = (me, (y + 1) % NY), (me, (y + NY - 1) % NY)
    greet([zup, zdn] + peer[1:] + [yup, ydn])

    lane = lax.broadcasted_iota(jnp.int32, (BLOCKS, 128), 1)
    wanted = jnp.zeros((BLOCKS, 128), jnp.int32)
    for j in range(NEIGH):
        wanted = wanted + jnp.where(owner_v[:, j : j + 1] == lane, row_v[:, j : j + 1], 0)
    tab_v[r] = jnp.sum(wanted, axis=0, keepdims=True)
    both = jnp.concatenate([kw[...].astype(F32), vw[...].astype(F32)], axis=0)
    wall[r, 0] = jnp.concatenate([both[:, :256], both[:, 256:]], axis=0).astype(BF16)

    tab_copies = [
        remote(tab_v.at[r], tab_v.at[r], tab_ss.at[t], tab_rs.at[t], peer[t])
        for t in range(1, PLANE)
    ]
    for copy in tab_copies:
        copy.start()

    def ring(s, way, part):
        bufs = (ups, dns)[way]
        piece = pl.ds(part * 8, 8)
        return remote(
            bufs[s].at[piece],
            bufs[s + 1].at[piece],
            ring_s.at[way, s, part],
            ring_r.at[way, s, part],
            (zup, zdn)[way],
        )

    def place(s, way):
        return 0 if s == 0 else 15 if s == 8 else 2 * s - 1 + way

    def weight_ring(s, way):
        return remote(
            wall.at[r, place(s, way)],
            wall.at[r, place(s + 1, way)],
            wring_s.at[way, s],
            wring_r.at[way, s],
            (zup, zdn)[way],
        )

    waits = []
    for s in range(9):
        ways = (0,) if s == 7 else (0, 1)
        if s > 0:
            for way in (0,) if s == 8 else (0, 1):
                weight_ring(s - 1, way).wait_recv()
        if s < 8:
            for way in ways:
                copy = weight_ring(s, way)
                copy.start()
                waits.append(copy)
        for part in range(2):
            for way in range(2):
                if s > 0 and not (s == 8 and part != way):
                    ring(s - 1, way, part).wait_recv()
                if s < 8 and not (s == 7 and part != way):
                    copy = ring(s, way, part)
                    copy.start()
                    waits.append(copy)
        if s == 0:
            for copy in tab_copies:
                copy.wait()
            local = pltpu.make_async_copy(tab_v, tab_s, tab_ls)
            local.start()
            local.wait()
        first, count = place(s, 0), 1 if s in (0, 8) else 2
        for n in range(count):
            buf = (ups, dns)[n][s]
            far = (z + NZ - s) % NZ if n == 0 else (z + s) % NZ
            for t in range(PLANE):
                entry = buf[tab_s[(r + t) % PLANE, 0, far * PLANE + r]]
                if t == 0:
                    got[r, first + n] = entry
                else:
                    stage[t, first + n] = entry
        cut = pl.ds(first, count)
        for t in range(1, PLANE):
            for copy in (
                remote(
                    wall.at[r, cut], wall.at[r, cut], wc_s.at[t, s], wc_r.at[t, s], peer[t]
                ),
                remote(
                    stage.at[t, cut], got.at[r, cut], cell_s.at[t, s], cell_r.at[t, s], peer[t]
                ),
            ):
                copy.start()
                waits.append(copy)
    for s in range(9):
        cut = pl.ds(place(s, 0), 1 if s in (0, 8) else 2)
        for t in range(1, PLANE):
            remote(
                stage.at[t, cut], got.at[r, cut], cell_s.at[t, s], cell_r.at[t, s], peer[t]
            ).wait_recv()

    y_copies = []
    for g in range(CHUNKS):
        for i in range(g * PER, (g + 1) * PER):
            o = owner_s[i // NEIGH, i % NEIGH]
            zo = o // PLANE
            rel = (zo - z + NZ) % NZ
            where_k = jnp.where(rel < 8, 2 * rel, 31 - 2 * rel)
            nb[y, i] = got[o % PLANE, where_k]
        piece = pl.ds(g * PER, PER)
        for way in range(2):
            copy = remote(
                nb.at[y, piece], nb.at[y, piece], ys_s.at[way, g], ys_r.at[way, g], (yup, ydn)[way]
            )
            copy.start()
            y_copies.append(copy)

    for s in range(9):
        cut = pl.ds(place(s, 0), 1 if s in (0, 8) else 2)
        for t in range(1, PLANE):
            remote(
                wall.at[r, cut], wall.at[r, cut], wc_s.at[t, s], wc_r.at[t, s], peer[t]
            ).wait_recv()
    line = lax.broadcasted_iota(jnp.int32, (64, 128), 0)
    column = lax.broadcasted_iota(jnp.int32, (64, 128), 1)
    line = (line % 32) // 4 * 16 + line // 32 * 4 + line % 4
    for k in range(16):
        if k == 0:
            zo = z
        elif k == 15:
            zo = (z + 8) % NZ
        else:
            d = (k + 1) // 2
            zo = (z + NZ - d) % NZ if k % 2 else (z + d) % NZ
        tiles = wall[:, k].reshape(128, 256)
        at = pl.ds(pl.multiple_of(zo * 32, 32), 32)
        for half in range(2):
            pick = jnp.where(line + half * 8 == column, 1.0, 0.0).astype(BF16)
            sorted_rows = jnp.dot(pick, tiles, preferred_element_type=F32).astype(BF16)
            wout[at, half * 256 : half * 256 + 256] = sorted_rows[:32]
            wout[at, WIDTH + half * 256 : WIDTH + half * 256 + 256] = sorted_rows[32:]

    forwards = []
    for g in range(CHUNKS):
        piece = pl.ds(g * PER, PER)
        way = g % 2
        for w in range(2):
            y_copies[2 * g + w].wait_recv()
        origin = (y + NY - 1) % NY if way == 0 else (y + 1) % NY
        copy = remote(
            nb.at[origin, piece], nb.at[origin, piece], yf_s.at[g], yf_r.at[g], (yup, ydn)[way]
        )
        copy.start()
        forwards.append(copy)
    for copy in waits + y_copies:
        copy.wait_send()
    for copy in forwards:
        copy.wait()


def fetch(store, key_weight, value_weight, owner, row):
    dma = pltpu.SemaphoreType.DMA
    return pl.pallas_call(
        fetch_kernel,
        out_shape=(
            jax.ShapeDtypeStruct((NY, SLOTS, NB_LEN, 128), BF16),
            jax.ShapeDtypeStruct((ENC_WIDTH, 2 * WIDTH), BF16),
        ),
        in_specs=[VSPEC] * 5 + [SSPEC],
        out_specs=(VSPEC, VSPEC),
        scratch_shapes=[VM((16, NB_LEN, 128), BF16)] * 15
        + [
            VM((PLANE, 1, 128), jnp.int32),
            pltpu.SMEM((PLANE, 1, 128), jnp.int32),
            VM((PLANE, 16, NB_LEN, 128), BF16),
            VM((PLANE, 16, NB_LEN, 128), BF16),
            VM((PLANE, 16, 16, 256), BF16),
            dma((2, 8, 2)),
            dma((2, 8, 2)),
            dma((2, 8)),
            dma((2, 8)),
            dma((PLANE, 9)),
            dma((PLANE, 9)),
            dma((PLANE, 9)),
            dma((PLANE, 9)),
            dma((PLANE,)),
            dma((PLANE,)),
            dma,
            dma((2, CHUNKS)),
            dma((2, CHUNKS)),
            dma((CHUNKS,)),
            dma((CHUNKS,)),
        ],
        compiler_params=pltpu.CompilerParams(
            collective_id=0, has_side_effects=True, vmem_limit_bytes=VLIMIT
        ),
    )(store, key_weight, value_weight, owner, row, owner)


def dot_t(a, b):
    return lax.dot_general(a, b, (((1,), (1,)), ((), ())), preferred_element_type=F32)


def t_dot(a, b):
    return lax.dot_general(a, b, (((0,), (0,)), ((), ())), preferred_element_type=F32)


def attend_kernel(nb, weights, queries, grads, valid, attended, cot, rows_t):
    factor = 1.0 / math.sqrt(HEAD_DIM)
    key_pos = lax.broadcasted_iota(jnp.int32, (1, NEIGH * NB_LEN), 1)

    for g in range(CHUNKS):
        rows = jnp.concatenate(
            [nb[f, g * PER : (g + 1) * PER].reshape(PER * NB_LEN, 128) for f in range(NY)], axis=1
        )
        rows_t[:, g * 256 : (g + 1) * 256] = rows.T
        states = jnp.dot(rows, weights[...], preferred_element_type=F32).astype(BF16)
        for b in range(2):
            block = 2 * g + b
            first, second = valid[block, 0], valid[block, 1]
            allowed = (key_pos < first) | ((key_pos >= NB_LEN) & (key_pos < NB_LEN + second))
            at = pl.ds(block * BLOCK_LEN, BLOCK_LEN)
            to = pl.ds(block * 128, 128)
            for h in range(HEADS_DEV):
                lanes = slice(h * 128, h * 128 + 128)
                key = states[b * 128 : b * 128 + 128, h * 128 : h * 128 + 128]
                value = states[b * 128 : b * 128 + 128, WIDTH + h * 128 : WIDTH + h * 128 + 128]
                query, grad = queries[at, lanes], grads[at, lanes]
                scores = jnp.where(allowed, factor * dot_t(query, key), -jnp.inf)
                exponent = jnp.exp(scores - jnp.max(scores, axis=1, keepdims=True))
                prob = exponent / jnp.sum(exponent, axis=1, keepdims=True)
                rounded = prob.astype(BF16)
                attended[at, lanes] = jnp.dot(
                    rounded, value, preferred_element_type=F32
                ).astype(BF16)
                grad_prob = dot_t(grad, value)
                inner = jnp.sum(prob * grad_prob, axis=1, keepdims=True)
                grad_score = (prob * (grad_prob - inner)).astype(BF16)
                cot[to, lanes] = (factor * t_dot(grad_score, query)).astype(BF16)
                cot[to, WIDTH + h * 128 : WIDTH + h * 128 + 128] = t_dot(rounded, grad).astype(BF16)


def attend(nb, weights, queries, grads, valid):
    return pl.pallas_call(
        attend_kernel,
        out_shape=(
            jax.ShapeDtypeStruct((BLOCKS * BLOCK_LEN, WIDTH), BF16),
            jax.ShapeDtypeStruct((ROWS, 2 * WIDTH), BF16),
            jax.ShapeDtypeStruct((ENC_WIDTH, ROWS), BF16),
        ),
        in_specs=[VSPEC] * 4 + [SSPEC],
        out_specs=(VSPEC,) * 3,
        compiler_params=pltpu.CompilerParams(vmem_limit_bytes=VLIMIT),
    )(nb, weights, queries, grads, valid)


def reduce_kernel(rows_t, cot, key_out, value_out, *scratch):
    c_send, c_recv, total, x_send, x_recv, own, z_send, z_recv, fin, fin_in = scratch[:10]
    cs, cr, xs, xr, zs, zr, fs, fr = scratch[10:]
    me = lax.axis_index("dp")
    y = lax.axis_index("mp")
    z, x, c = me // PLANE, (me % PLANE) // 2, me % 2
    mate = (me + 1 - 2 * c, y)
    x_peer = [(z * PLANE + ((x + t) % NX) * 2 + c, y) for t in range(1, NX)]
    z_peer = [(((z + t) % NZ) * PLANE + x * 2 + c, y) for t in range(1, NZ)]
    greet([mate] + x_peer + z_peer)

    core_copies, x_copies, z_copies = [], [], []
    for h in range(2):
        theirs = pl.ds(pl.multiple_of((1 - c) * WIDTH + h * 256, 128), 256)
        mine = pl.ds(pl.multiple_of(c * WIDTH + h * 256, 128), 256)
        c_send[h] = jnp.dot(rows_t[...], cot[:, theirs], preferred_element_type=F32)
        copy = remote(c_send.at[h], c_recv.at[h], cs.at[h], cr.at[h], mate)
        copy.start()
        core_copies.append(copy)
        total[h] = jnp.dot(
            rows_t[...], cot[:, mine], preferred_element_type=F32
        ).reshape(NZ, NX, 8, 256)
    for h in range(2):
        core_copies[h].wait_recv()
        total[h] = total[h] + c_recv[h].reshape(NZ, NX, 8, 256)
        for t in range(1, NX):
            x_send[h, t - 1] = total[h, :, (x + t) % NX].reshape(128, 256).astype(BF16)
            copy = remote(
                x_send.at[h, t - 1], x_recv.at[h, t - 1], xs.at[h, t - 1], xr.at[h, t - 1], x_peer[t - 1]
            )
            copy.start()
            x_copies.append(copy)
    for h in range(2):
        line_sum = total[h, :, x]
        for t in range(1, NX):
            x_copies[h * 3 + t - 1].wait_recv()
            line_sum = line_sum + x_recv[h, t - 1].astype(F32).reshape(NZ, 8, 256)
        line_sum = jnp.concatenate([line_sum[:, :, :128], line_sum[:, :, 128:]], axis=1)
        own[h] = line_sum
        z_send[h] = line_sum.astype(BF16)
        for t in range(1, NZ):
            copy = remote(
                z_send.at[h, (z + t) % NZ],
                z_recv.at[h, t - 1],
                zs.at[h, t - 1],
                zr.at[h, t - 1],
                z_peer[t - 1],
            )
            copy.start()
            z_copies.append(copy)
    for h in range(2):
        done = own[h, z]
        for t in range(1, NZ):
            z_copies[h * 15 + t - 1].wait_recv()
            done = done + z_recv[h, t - 1].astype(F32)
        fin[:, h * 256 : h * 256 + 128] = done[:8]
        fin[:, h * 256 + 128 : h * 256 + 256] = done[8:]
    last = remote(fin, fin_in, fs, fr, mate)
    last.start()
    for copy in core_copies + x_copies + z_copies:
        copy.wait_send()
    last.wait()
    even = c == 0
    mine = jnp.where(even, fin[:4], fin[4:])
    theirs = jnp.where(even, fin_in[:4], fin_in[4:])
    key_out[...] = jnp.where(even, mine, theirs)
    value_out[...] = jnp.where(even, theirs, mine)


def reduce(rows_t, cot):
    dma = pltpu.SemaphoreType.DMA
    return pl.pallas_call(
        reduce_kernel,
        out_shape=(jax.ShapeDtypeStruct((4, WIDTH), F32),) * 2,
        in_specs=[VSPEC] * 2,
        out_specs=(VSPEC,) * 2,
        scratch_shapes=[
            VM((2, ENC_WIDTH, 256), F32),
            VM((2, ENC_WIDTH, 256), F32),
            VM((2, NZ, NX, 8, 256), F32),
            VM((2, NX - 1, 128, 256), BF16),
            VM((2, NX - 1, 128, 256), BF16),
            VM((2, NZ, 16, 128), F32),
            VM((2, NZ, 16, 128), BF16),
            VM((2, NZ - 1, 16, 128), BF16),
            VM((8, WIDTH), F32),
            VM((8, WIDTH), F32),
            dma((2,)),
            dma((2,)),
            dma((2, NX - 1)),
            dma((2, NX - 1)),
            dma((2, NZ - 1)),
            dma((2, NZ - 1)),
            dma,
            dma,
        ],
        compiler_params=pltpu.CompilerParams(
            collective_id=1, has_side_effects=True, vmem_limit_bytes=VLIMIT
        ),
    )(rows_t, cot)


def shards(queries, out_grad, store, key_weight, value_weight, owner, row, valid):
    nb, weights = fetch(store, key_weight, value_weight, owner, row)
    attended, cot, rows_t = attend(nb, weights, queries, out_grad, valid)
    key_grad, value_grad = reduce(rows_t, cot)
    return attended, key_grad, value_grad


def solution(mesh):
    in_specs = (
        P("dp", "mp"),
        P("dp", "mp"),
        P("dp", None, "mp"),
        P("dp", "mp"),
        P("dp", "mp"),
        P("dp", None),
        P("dp", None),
        P("dp", None),
    )
    out_specs = (P("dp", "mp"), P("dp", "mp"), P("dp", "mp"))
    return jax.shard_map(shards, mesh=mesh, in_specs=in_specs, out_specs=out_specs, check_vma=False)
```

```python
import functools
import math

import jax
import jax.numpy as jnp
from jax import lax
from jax.experimental import pallas as pl
from jax.experimental.pallas import tpu as pltpu
from jax.sharding import PartitionSpec as P

HEAD_DIM = 128
ENC_WIDTH = 512
BLOCK_LEN = 64
NEIGH = 2
NB_LEN = 64
BLOCKS = 14
SLOTS = BLOCKS * NEIGH
ROWS = SLOTS * NB_LEN
HEADS_DEV = 4
WIDTH = HEADS_DEV * HEAD_DIM
NZ, NX, NY, PLANE = 16, 4, 4, 8
CHUNKS = 7
PER = SLOTS // CHUNKS

MESH = pl.DeviceIdType.MESH
F32 = jnp.float32
BF16 = jnp.bfloat16
VM = pltpu.VMEM
VSPEC = pl.BlockSpec(memory_space=pltpu.VMEM)
SSPEC = pl.BlockSpec(memory_space=pltpu.SMEM)
VLIMIT = 56 * 2**20


def remote(src, dst, send, recv, device):
    return pltpu.make_async_remote_copy(
        src_ref=src,
        dst_ref=dst,
        send_sem=send,
        recv_sem=recv,
        device_id=device,
        device_id_type=MESH,
    )


def greet(devices):
    barrier = pltpu.get_barrier_semaphore()
    for device in devices:
        pl.semaphore_signal(barrier, inc=1, device_id=device, device_id_type=MESH)
    pl.semaphore_wait(barrier, len(devices))


def dot(a, b):
    return jnp.dot(a, b, preferred_element_type=F32)


def dot_t(a, b):
    return lax.dot_general(a, b, (((1,), (1,)), ((), ())), preferred_element_type=F32)


def attend_chunk(g, nb, weights, queries, grads, valid, attended, cot, rows_t):
    factor = 1.0 / math.sqrt(HEAD_DIM)
    rows = jnp.concatenate(
        [nb[f, g * PER : (g + 1) * PER].reshape(PER * NB_LEN, 128) for f in range(NY)], axis=1
    )
    states = dot(rows, weights[...]).astype(BF16)
    rows_t[:, g * 256 : (g + 1) * 256] = rows.T
    key_pos = lax.broadcasted_iota(jnp.int32, (NEIGH * NB_LEN, 2 * BLOCK_LEN), 0)
    zero = jnp.zeros((BLOCK_LEN, HEAD_DIM), BF16)

    def diagonal(ref, at, lane):
        return jnp.concatenate(
            [
                jnp.concatenate([ref[at, lane : lane + 128], zero], axis=1),
                jnp.concatenate([zero, ref[at, lane + 128 : lane + 256]], axis=1),
            ],
            axis=0,
        )

    for b in range(2):
        block = 2 * g + b
        first, second = valid[0, block], valid[1, block]
        allowed = (key_pos < first) | ((key_pos >= NB_LEN) & (key_pos < NB_LEN + second))
        at = slice(block * BLOCK_LEN, (block + 1) * BLOCK_LEN)
        to = slice(block * 128, block * 128 + 128)
        for lane in range(0, WIDTH, 256):
            key = states[b * 128 : b * 128 + 128, lane : lane + 256]
            value = states[b * 128 : b * 128 + 128, WIDTH + lane : WIDTH + lane + 256]
            query, grad = diagonal(queries, at, lane), diagonal(grads, at, lane)
            scores = jnp.where(allowed, factor * dot_t(key, query), -jnp.inf)
            exponent = jnp.exp(scores - jnp.max(scores, axis=0, keepdims=True))
            prob = exponent * (1.0 / jnp.sum(exponent, axis=0, keepdims=True))
            rounded = prob.astype(BF16)
            out = dot(rounded.T, value).astype(BF16)
            attended[at, lane : lane + 128] = out[:BLOCK_LEN, :128]
            attended[at, lane + 128 : lane + 256] = out[BLOCK_LEN:, 128:]
            grad_prob = dot_t(value, grad)
            inner = jnp.sum(prob * grad_prob, axis=0, keepdims=True)
            grad_score = (prob * (grad_prob - inner)).astype(BF16)
            cot[to, lane : lane + 256] = (factor * dot(grad_score, query)).astype(BF16)
            cot[to, WIDTH + lane : WIDTH + lane + 256] = dot(rounded, grad).astype(BF16)


def step_kernel(names, *refs):
    (store, kw, vw, owner_s, row_s, valid_s, queries_h, grads_h, attended_h, sums_out) = refs[:10]
    planes, named = refs[10:25], dict(zip(names, refs[25:]))
    S = lambda name: named[name]
    tab_v, tab_s, stage, got, wall = map(S, ("tab_v", "tab_s", "stage", "got", "wall"))
    nb, weights, queries, grads, attended = map(S, ("nb", "weights", "queries", "grads", "attended"))
    ups = [store] + [planes[2 * s - 2] for s in range(1, 8)] + [planes[14]]
    dns = [store] + [planes[2 * s - 1] for s in range(1, 8)] + [planes[14]]
    me = lax.axis_index("dp")
    y = lax.axis_index("mp")
    z, r = me // PLANE, me % PLANE
    x, c = r // 2, r % 2
    zup = (((z + 1) % NZ) * PLANE + r, y)
    zdn = (((z + NZ - 1) % NZ) * PLANE + r, y)
    peer = [(z * PLANE + (r + t) % PLANE, y) for t in range(PLANE)]
    yup, ydn = (me, (y + 1) % NY), (me, (y + NY - 1) % NY)
    mate = (me + 1 - 2 * c, y)
    x_peer = [(z * PLANE + ((x + t) % NX) * 2 + c, y) for t in range(1, NX)]
    z_peer = [(((z + t) % NZ) * PLANE + r, y) for t in range(1, NZ)]

    local_sem = S("local_sem")
    loads = [
        pltpu.make_async_copy(queries_h, queries, local_sem.at[0]),
        pltpu.make_async_copy(grads_h, grads, local_sem.at[1]),
    ]
    for copy in loads:
        copy.start()
    greet(peer[1:] + z_peer + [yup, ydn])

    lane = lax.broadcasted_iota(jnp.int32, (1, 128), 1)
    wanted = jnp.zeros((1, 128), jnp.int32)
    for j in range(NEIGH):
        for b in range(BLOCKS):
            wanted = wanted + jnp.where(lane == owner_s[j, b], row_s[j, b], 0)
    tab_v[r] = wanted
    both = jnp.concatenate([kw[...].astype(F32), vw[...].astype(F32)], axis=0)
    wall[r, 0] = jnp.concatenate([both[:, :256], both[:, 256:]], axis=0).astype(BF16)

    tab_copies = [
        remote(tab_v.at[r], tab_v.at[r], S("tab_ss").at[t], S("tab_rs").at[t], peer[t])
        for t in range(1, PLANE)
    ]
    for copy in tab_copies:
        copy.start()

    def ring(s, way, part):
        bufs = (ups, dns)[way]
        piece = pl.ds(part * 8, 8)
        return remote(
            bufs[s].at[piece],
            bufs[s + 1].at[piece],
            S("ring_s").at[way, s, part],
            S("ring_r").at[way, s, part],
            (zup, zdn)[way],
        )

    def place(s, way):
        return 0 if s == 0 else 15 if s == 8 else 2 * s - 1 + way

    def cut_of(s):
        return pl.ds(place(s, 0), 1 if s in (0, 8) else 2)

    def weight_ring(s, way):
        return remote(
            wall.at[r, place(s, way)],
            wall.at[r, place(s + 1, way)],
            S("wring_s").at[way, s],
            S("wring_r").at[way, s],
            (zup, zdn)[way],
        )

    def weight_plane(s, t):
        rows = wall.at[r, cut_of(s)]
        return remote(rows, rows, S("wc_s").at[t, s], S("wc_r").at[t, s], peer[t])

    def cell_plane(s, t):
        return remote(
            stage.at[t, cut_of(s)],
            got.at[r, cut_of(s)],
            S("cell_s").at[t, s],
            S("cell_r").at[t, s],
            peer[t],
        )

    line = lax.broadcasted_iota(jnp.int32, (64, 128), 0)
    column = lax.broadcasted_iota(jnp.int32, (64, 128), 1)
    line = (line % 32) // 4 * 16 + line // 32 * 4 + line % 4
    picks = [jnp.where(line + half * 8 == column, 1.0, 0.0).astype(BF16) for half in range(2)]

    def place_weights(s):
        for t in range(1, PLANE):
            weight_plane(s, t).wait_recv()
        for way in range(1 if s in (0, 8) else 2):
            far = (z + NZ - s) % NZ if way == 0 else (z + s) % NZ
            tiles = wall[:, place(s, way)].reshape(128, 256)
            at = pl.ds(pl.multiple_of(far * 32, 32), 32)
            for half in range(2):
                ordered = dot(picks[half], tiles).astype(BF16)
                weights[at, half * 256 : half * 256 + 256] = ordered[:32]
                weights[at, WIDTH + half * 256 : WIDTH + half * 256 + 256] = ordered[32:]

    sent = []
    for s in range(9):
        if s > 0:
            for way in (0,) if s == 8 else (0, 1):
                weight_ring(s - 1, way).wait_recv()
        if s < 8:
            for way in (0,) if s == 7 else (0, 1):
                copy = weight_ring(s, way)
                copy.start()
                sent.append(copy)
        for part in range(2):
            for way in range(2):
                if s > 0 and not (s == 8 and part != way):
                    ring(s - 1, way, part).wait_recv()
                if s < 8 and not (s == 7 and part != way):
                    copy = ring(s, way, part)
                    copy.start()
                    sent.append(copy)
        if s == 0:
            for copy in tab_copies:
                copy.wait()
            local = pltpu.make_async_copy(tab_v, tab_s, local_sem.at[2])
            local.start()
            local.wait()
        for way in range(1 if s in (0, 8) else 2):
            buf = (ups, dns)[way][s]
            far = (z + NZ - s) % NZ if way == 0 else (z + s) % NZ
            for t in range(PLANE):
                entry = buf[tab_s[(r + t) % PLANE, 0, far * PLANE + r]]
                if t == 0:
                    got[r, place(s, way)] = entry
                else:
                    stage[t, place(s, way)] = entry
        for t in range(1, PLANE):
            for copy in (weight_plane(s, t), cell_plane(s, t)):
                copy.start()
                sent.append(copy)
        if s >= 2:
            place_weights(s - 2)
    place_weights(7)
    for s in range(9):
        for t in range(1, PLANE):
            cell_plane(s, t).wait_recv()

    def own_y(g, way):
        part = nb.at[y, pl.ds(g * PER, PER)]
        return remote(part, part, S("ys_s").at[way, g], S("ys_r").at[way, g], (yup, ydn)[way])

    def forward_y(g):
        origin = (y + NY - 1) % NY if g % 2 == 0 else (y + 1) % NY
        part = nb.at[origin, pl.ds(g * PER, PER)]
        return remote(part, part, S("yf_s").at[g], S("yf_r").at[g], (yup, ydn)[g % 2])

    def send_own(g):
        for i in range(g * PER, (g + 1) * PER):
            o = owner_s[i % NEIGH, i // NEIGH]
            rel = (o // PLANE - z + NZ) % NZ
            nb[y, i] = got[o % PLANE, jnp.where(rel < 8, 2 * rel, 31 - 2 * rel)]
        for way in range(2):
            copy = own_y(g, way)
            copy.start()
            sent.append(copy)

    ahead = 3
    for g in range(ahead):
        send_own(g)
    place_weights(8)
    for copy in loads:
        copy.wait()
    stores = []

    def attend(g):
        forward_y(g).wait_recv()
        attend_chunk(
            g, nb, weights, queries, grads, valid_s, attended, S("cot"), S("rows_t")
        )
        piece = pl.ds(g * 128, 128)
        copy = pltpu.make_async_copy(
            attended.at[piece], attended_h.at[piece], S("out_sem").at[g]
        )
        copy.start()
        stores.append(copy)

    for g in range(CHUNKS):
        for way in range(2):
            own_y(g, way).wait_recv()
        copy = forward_y(g)
        copy.start()
        sent.append(copy)
        if g + ahead < CHUNKS:
            send_own(g + ahead)
        if g > 0:
            attend(g - 1)
    attend(CHUNKS - 1)

    rows_t, cot, total = S("rows_t"), S("cot"), S("total")
    c_send, c_recv, x_send, x_recv = map(S, ("c_send", "c_recv", "x_send", "x_recv"))
    own, z_send, z_recv = map(S, ("own", "z_send", "z_recv"))
    core_copies, x_copies, z_copies = [], [], []
    for h in range(2):
        theirs = pl.ds(pl.multiple_of((1 - c) * WIDTH + h * 256, 128), 256)
        c_send[h] = dot(rows_t[...], cot[:, theirs]).astype(BF16)
        copy = remote(c_send.at[h], c_recv.at[h], S("cs").at[h], S("cr").at[h], mate)
        copy.start()
        core_copies.append(copy)
    for h in range(2):
        mine = pl.ds(pl.multiple_of(c * WIDTH + h * 256, 128), 256)
        part = dot(rows_t[...], cot[:, mine])
        core_copies[h].wait_recv()
        total[h] = (part + c_recv[h].astype(F32)).reshape(NZ, NX, 8, 256)
        for t in range(1, NX):
            x_send[h, t - 1] = total[h, :, (x + t) % NX].reshape(128, 256).astype(BF16)
            copy = remote(
                x_send.at[h, t - 1],
                x_recv.at[h, t - 1],
                S("xs").at[h, t - 1],
                S("xr").at[h, t - 1],
                x_peer[t - 1],
            )
            copy.start()
            x_copies.append(copy)
    for h in range(2):
        line_sum = total[h, :, x]
        for t in range(1, NX):
            x_copies[h * 3 + t - 1].wait_recv()
            line_sum = line_sum + x_recv[h, t - 1].astype(F32).reshape(NZ, 8, 256)
        line_sum = jnp.concatenate([line_sum[:, :, :128], line_sum[:, :, 128:]], axis=1)
        own[h] = line_sum
        z_send[h] = line_sum.astype(BF16)
        for t in range(1, NZ):
            copy = remote(
                z_send.at[h, (z + t) % NZ],
                z_recv.at[h, t - 1],
                S("zs").at[h, t - 1],
                S("zr").at[h, t - 1],
                z_peer[t - 1],
            )
            copy.start()
            z_copies.append(copy)
    fin, fin_in = S("fin"), S("fin_in")
    for h in range(2):
        done = own[h, z]
        for t in range(1, NZ):
            z_copies[h * 15 + t - 1].wait_recv()
            done = done + z_recv[h, t - 1].astype(F32)
        fin[:, h * 256 : h * 256 + 128] = done[:8]
        fin[:, h * 256 + 128 : h * 256 + 256] = done[8:]
    last = remote(fin, fin_in, S("fs"), S("fr"), mate)
    last.start()
    for copy in sent + core_copies + x_copies + z_copies:
        copy.wait_send()
    for copy in stores:
        copy.wait()
    last.wait()
    even = c == 0
    sums_out[0] = jnp.where(even, fin[...], fin_in[...])
    sums_out[1] = jnp.where(even, fin_in[...], fin[...])


def step(queries, out_grad, store, key_weight, value_weight, owner, row, valid):
    dma = pltpu.SemaphoreType.DMA
    scratch = {
        "tab_v": VM((PLANE, 1, 128), jnp.int32),
        "tab_s": pltpu.SMEM((PLANE, 1, 128), jnp.int32),
        "stage": VM((PLANE, 16, NB_LEN, 128), BF16),
        "got": VM((PLANE, 16, NB_LEN, 128), BF16),
        "wall": VM((PLANE, 16, 16, 256), BF16),
        "nb": VM((NY, SLOTS, NB_LEN, 128), BF16),
        "weights": VM((ENC_WIDTH, 2 * WIDTH), BF16),
        "queries": VM((BLOCKS * BLOCK_LEN, WIDTH), BF16),
        "grads": VM((BLOCKS * BLOCK_LEN, WIDTH), BF16),
        "attended": VM((BLOCKS * BLOCK_LEN, WIDTH), BF16),
        "cot": VM((ROWS, 2 * WIDTH), BF16),
        "rows_t": VM((ENC_WIDTH, ROWS), BF16),
        "c_send": VM((2, ENC_WIDTH, 256), BF16),
        "c_recv": VM((2, ENC_WIDTH, 256), BF16),
        "total": VM((2, NZ, NX, 8, 256), F32),
        "x_send": VM((2, NX - 1, 128, 256), BF16),
        "x_recv": VM((2, NX - 1, 128, 256), BF16),
        "own": VM((2, NZ, 16, 128), F32),
        "z_send": VM((2, NZ, 16, 128), BF16),
        "z_recv": VM((2, NZ - 1, 16, 128), BF16),
        "fin": VM((8, WIDTH), F32),
        "fin_in": VM((8, WIDTH), F32),
        "local_sem": dma((3,)),
        "out_sem": dma((CHUNKS,)),
        "fs": dma,
        "fr": dma,
    }
    for send, recv, shape in (
        ("ring_s", "ring_r", (2, 8, 2)),
        ("wring_s", "wring_r", (2, 8)),
        ("cell_s", "cell_r", (PLANE, 9)),
        ("wc_s", "wc_r", (PLANE, 9)),
        ("tab_ss", "tab_rs", (PLANE,)),
        ("ys_s", "ys_r", (2, CHUNKS)),
        ("yf_s", "yf_r", (CHUNKS,)),
        ("cs", "cr", (2,)),
        ("xs", "xr", (2, NX - 1)),
        ("zs", "zr", (2, NZ - 1)),
    ):
        scratch[send] = dma(shape)
        scratch[recv] = dma(shape)
    anywhere = pl.BlockSpec(memory_space=pl.ANY)
    return pl.pallas_call(
        functools.partial(step_kernel, tuple(scratch)),
        out_shape=(
            jax.ShapeDtypeStruct((BLOCKS * BLOCK_LEN, WIDTH), BF16),
            jax.ShapeDtypeStruct((2, 8, WIDTH), F32),
        ),
        in_specs=[VSPEC] * 3 + [SSPEC] * 3 + [anywhere] * 2,
        out_specs=(anywhere, VSPEC),
        scratch_shapes=[VM((16, NB_LEN, 128), BF16)] * 15 + list(scratch.values()),
        compiler_params=pltpu.CompilerParams(
            collective_id=0, has_side_effects=True, vmem_limit_bytes=VLIMIT
        ),
    )(store, key_weight, value_weight, owner.T, row.T, valid.T, queries, out_grad)


def finish_kernel(attended_in, sums, attended, key_out, value_out, held, sem_in, sem_out):
    count = sem_in.shape[0]
    size = held.shape[0] // count
    pieces = [pl.ds(i * size, size) for i in range(count)]
    inward = [
        pltpu.make_async_copy(attended_in.at[piece], held.at[piece], sem_in.at[i])
        for i, piece in enumerate(pieces)
    ]
    outward = [
        pltpu.make_async_copy(held.at[piece], attended.at[piece], sem_out.at[i])
        for i, piece in enumerate(pieces)
    ]
    for copy in inward:
        copy.start()
    low = lax.axis_index("dp") % 2 == 0
    key_out[...] = jnp.where(low, sums[0, :4], sums[0, 4:])
    value_out[...] = jnp.where(low, sums[1, :4], sums[1, 4:])
    for i in range(count):
        inward[i].wait()
        outward[i].start()
    for copy in outward:
        copy.wait()


def finish(attended, sums):
    anywhere = pl.BlockSpec(memory_space=pl.ANY)
    dma = pltpu.SemaphoreType.DMA
    return pl.pallas_call(
        finish_kernel,
        out_shape=(
            jax.ShapeDtypeStruct(attended.shape, BF16),
            jax.ShapeDtypeStruct((4, WIDTH), F32),
            jax.ShapeDtypeStruct((4, WIDTH), F32),
        ),
        in_specs=[anywhere, VSPEC],
        out_specs=(anywhere, VSPEC, VSPEC),
        scratch_shapes=[VM(attended.shape, BF16), dma((CHUNKS,)), dma((CHUNKS,))],
        compiler_params=pltpu.CompilerParams(vmem_limit_bytes=VLIMIT),
    )(attended, sums)


def shards(queries, out_grad, store, key_weight, value_weight, owner, row, valid):
    attended, sums = step(
        queries, out_grad, store, key_weight, value_weight, owner, row, valid
    )
    return finish(attended, sums)


def solution(mesh):
    in_specs = (
        P("dp", "mp"),
        P("dp", "mp"),
        P("dp", None, "mp"),
        P("dp", "mp"),
        P("dp", "mp"),
        P("dp", None),
        P("dp", None),
        P("dp", None),
    )
    out_specs = (P("dp", "mp"), P("dp", "mp"), P("dp", "mp"))
    return jax.shard_map(shards, mesh=mesh, in_specs=in_specs, out_specs=out_specs, check_vma=False)
```

```python
import functools
import math

import jax
import jax.numpy as jnp
from jax import lax
from jax.experimental import pallas as pl
from jax.experimental.pallas import tpu as pltpu
from jax.sharding import PartitionSpec as P

HEAD_DIM = 128
ENC_WIDTH = 512
BLOCK_LEN = 64
NEIGH = 2
NB_LEN = 64
BLOCKS = 14
SLOTS = BLOCKS * NEIGH
ROWS = SLOTS * NB_LEN
HEADS_DEV = 4
WIDTH = HEADS_DEV * HEAD_DIM
NZ, NX, NY, PLANE = 16, 4, 4, 8
CHUNKS = 7
FAR_FIRST = (4, 5, 2, 3, 6, 7, 1, 0)
PER = SLOTS // CHUNKS

MESH = pl.DeviceIdType.MESH
F32 = jnp.float32
BF16 = jnp.bfloat16
VM = pltpu.VMEM
VSPEC = pl.BlockSpec(memory_space=pltpu.VMEM)
SSPEC = pl.BlockSpec(memory_space=pltpu.SMEM)
VLIMIT = 56 * 2**20


def remote(src, dst, send, recv, device):
    return pltpu.make_async_remote_copy(
        src_ref=src,
        dst_ref=dst,
        send_sem=send,
        recv_sem=recv,
        device_id=device,
        device_id_type=MESH,
    )


def greet(devices):
    barrier = pltpu.get_barrier_semaphore()
    for device in devices:
        pl.semaphore_signal(barrier, inc=1, device_id=device, device_id_type=MESH)
    pl.semaphore_wait(barrier, len(devices))


def dot(a, b):
    return jnp.dot(a, b, preferred_element_type=F32)


def dot_t(a, b):
    return lax.dot_general(a, b, (((1,), (1,)), ((), ())), preferred_element_type=F32)


def attend_chunk(g, nb, weights, queries, grads, valid, attended, cot, rows_t):
    factor = 1.0 / math.sqrt(HEAD_DIM)
    rows = jnp.concatenate(
        [nb[f, g * PER : (g + 1) * PER].reshape(PER * NB_LEN, 128) for f in range(NY)], axis=1
    )
    states = dot(rows, weights[...]).astype(BF16)
    rows_t[:, g * 256 : (g + 1) * 256] = rows.T
    key_pos = lax.broadcasted_iota(jnp.int32, (NEIGH * NB_LEN, 2 * BLOCK_LEN), 0)
    zero = jnp.zeros((BLOCK_LEN, HEAD_DIM), BF16)

    def diagonal(ref, at, lane):
        return jnp.concatenate(
            [
                jnp.concatenate([ref[at, lane : lane + 128], zero], axis=1),
                jnp.concatenate([zero, ref[at, lane + 128 : lane + 256]], axis=1),
            ],
            axis=0,
        )

    for b in range(2):
        block = 2 * g + b
        first, second = valid[0, block], valid[1, block]
        allowed = (key_pos < first) | ((key_pos >= NB_LEN) & (key_pos < NB_LEN + second))
        at = slice(block * BLOCK_LEN, (block + 1) * BLOCK_LEN)
        to = slice(block * 128, block * 128 + 128)
        for lane in range(0, WIDTH, 256):
            key = states[b * 128 : b * 128 + 128, lane : lane + 256]
            value = states[b * 128 : b * 128 + 128, WIDTH + lane : WIDTH + lane + 256]
            query, grad = diagonal(queries, at, lane), diagonal(grads, at, lane)
            scores = jnp.where(allowed, factor * dot_t(key, query), -jnp.inf)
            exponent = jnp.exp(scores - jnp.max(scores, axis=0, keepdims=True))
            prob = exponent * (1.0 / jnp.sum(exponent, axis=0, keepdims=True))
            rounded = prob.astype(BF16)
            out = dot(rounded.T, value).astype(BF16)
            attended[at, lane : lane + 128] = out[:BLOCK_LEN, :128]
            attended[at, lane + 128 : lane + 256] = out[BLOCK_LEN:, 128:]
            grad_prob = dot_t(value, grad)
            inner = jnp.sum(prob * grad_prob, axis=0, keepdims=True)
            grad_score = (prob * (grad_prob - inner)).astype(BF16)
            cot[to, lane : lane + 256] = (factor * dot(grad_score, query)).astype(BF16)
            cot[to, WIDTH + lane : WIDTH + lane + 256] = dot(rounded, grad).astype(BF16)


def step_kernel(names, *refs):
    (store_h, kw, vw, owner_s, row_s, valid_s, queries_h, grads_h, attended_h, sums_h) = refs[:10]
    planes, named = refs[10:25], dict(zip(names, refs[25:]))
    S = named.__getitem__
    store = S("store")
    tab_v, tab_s, stage, got, wall = map(S, ("tab_v", "tab_s", "stage", "got", "wall"))
    nb, weights, queries, grads, attended = map(S, ("nb", "weights", "queries", "grads", "attended"))
    ups = [store] + [planes[2 * s - 2] for s in range(1, 8)] + [planes[14]]
    dns = [store] + [planes[2 * s - 1] for s in range(1, 8)] + [planes[14]]
    me = lax.axis_index("dp")
    y = lax.axis_index("mp")
    z, r = me // PLANE, me % PLANE
    x, c = r // 2, r % 2
    zup = (((z + 1) % NZ) * PLANE + r, y)
    zdn = (((z + NZ - 1) % NZ) * PLANE + r, y)
    peer = [(z * PLANE + (r + t) % PLANE, y) for t in range(PLANE)]
    yup, ydn = (me, (y + 1) % NY), (me, (y + NY - 1) % NY)
    mate = (me + 1 - 2 * c, y)
    x_peer = [(z * PLANE + ((x + t) % NX) * 2 + c, y) for t in range(1, NX)]
    z_peer = [(((z + t) % NZ) * PLANE + r, y) for t in range(1, NZ)]

    local_sem = S("local_sem")
    load_store = pltpu.make_async_copy(store_h, store, local_sem.at[3])
    load_store.start()
    loads = [
        pltpu.make_async_copy(queries_h, queries, local_sem.at[0]),
        pltpu.make_async_copy(grads_h, grads, local_sem.at[1]),
    ]
    for copy in loads:
        copy.start()
    greet([zup, zdn, yup, ydn] + peer[1:])
    load_store.wait()

    lane = lax.broadcasted_iota(jnp.int32, (1, 128), 1)
    wanted = jnp.zeros((1, 128), jnp.int32)
    for j in range(NEIGH):
        for b in range(BLOCKS):
            wanted = wanted + jnp.where(lane == owner_s[j, b], row_s[j, b], 0)
    tab_v[r] = wanted
    both = jnp.concatenate([kw[...].astype(F32), vw[...].astype(F32)], axis=0)
    wall[r, 0] = jnp.concatenate([both[:, :256], both[:, 256:]], axis=0).astype(BF16)

    tab_copies = [
        remote(tab_v.at[r], tab_v.at[r], S("tab_ss").at[t], S("tab_rs").at[t], peer[t])
        for t in range(1, PLANE)
    ]
    for copy in tab_copies:
        copy.start()

    def ring(s, way, part):
        bufs = (ups, dns)[way]
        piece = pl.ds(part * 8, 8)
        return remote(
            bufs[s].at[piece],
            bufs[s + 1].at[piece],
            S("ring_s").at[way, s, part],
            S("ring_r").at[way, s, part],
            (zup, zdn)[way],
        )

    def place(s, way):
        return 0 if s == 0 else 15 if s == 8 else 2 * s - 1 + way

    def cut_of(s):
        return pl.ds(place(s, 0), 1 if s in (0, 8) else 2)

    def weight_ring(s, way):
        return remote(
            wall.at[r, place(s, way)],
            wall.at[r, place(s + 1, way)],
            S("wring_s").at[way, s],
            S("wring_r").at[way, s],
            (zup, zdn)[way],
        )

    def weight_plane(s, t):
        rows = wall.at[r, cut_of(s)]
        return remote(rows, rows, S("wc_s").at[t, s], S("wc_r").at[t, s], peer[t])

    def cell_plane(s, t):
        return remote(
            stage.at[t, cut_of(s)],
            got.at[r, cut_of(s)],
            S("cell_s").at[t, s],
            S("cell_r").at[t, s],
            peer[t],
        )

    line = lax.broadcasted_iota(jnp.int32, (64, 128), 0)
    column = lax.broadcasted_iota(jnp.int32, (64, 128), 1)
    line = (line % 32) // 4 * 16 + line // 32 * 4 + line % 4
    picks = [jnp.where(line + half * 8 == column, 1.0, 0.0).astype(BF16) for half in range(2)]

    def place_weights(s):
        for t in range(1, PLANE):
            weight_plane(s, t).wait_recv()
        for way in range(1 if s in (0, 8) else 2):
            far = (z + NZ - s) % NZ if way == 0 else (z + s) % NZ
            tiles = wall[:, place(s, way)].reshape(128, 256)
            at = pl.ds(pl.multiple_of(far * 32, 32), 32)
            for half in range(2):
                ordered = dot(picks[half], tiles).astype(BF16)
                weights[at, half * 256 : half * 256 + 256] = ordered[:32]
                weights[at, WIDTH + half * 256 : WIDTH + half * 256 + 256] = ordered[32:]

    sent = []
    for s in range(9):
        if s > 0:
            for way in (0,) if s == 8 else (0, 1):
                weight_ring(s - 1, way).wait_recv()
        if s < 8:
            for way in (0,) if s == 7 else (0, 1):
                copy = weight_ring(s, way)
                copy.start()
                sent.append(copy)
        for part in range(2):
            for way in range(2):
                if s > 0 and not (s == 8 and part != way):
                    ring(s - 1, way, part).wait_recv()
                if s < 8 and not (s == 7 and part != way):
                    copy = ring(s, way, part)
                    copy.start()
                    sent.append(copy)
        if s == 0:
            for copy in tab_copies:
                copy.wait()
            local = pltpu.make_async_copy(tab_v, tab_s, local_sem.at[2])
            local.start()
            local.wait()
        for t in FAR_FIRST:
            for way in range(1 if s in (0, 8) else 2):
                buf = (ups, dns)[way][s]
                far = (z + NZ - s) % NZ if way == 0 else (z + s) % NZ
                entry = buf[tab_s[(r + t) % PLANE, 0, far * PLANE + r]]
                if t == 0:
                    got[r, place(s, way)] = entry
                else:
                    stage[t, place(s, way)] = entry
            if t > 0:
                copy = cell_plane(s, t)
                copy.start()
                sent.append(copy)
        for late in () if s == 0 else (s - 1,) if s < 8 else (7, 8):
            for t in range(1, PLANE):
                copy = weight_plane(late, t)
                copy.start()
                sent.append(copy)
        if s >= 3:
            place_weights(s - 3)
    for s in range(9):
        for t in range(1, PLANE):
            cell_plane(s, t).wait_recv()

    def own_y(g, way):
        part = nb.at[y, pl.ds(g * PER, PER)]
        return remote(part, part, S("ys_s").at[way, g], S("ys_r").at[way, g], (yup, ydn)[way])

    def forward_y(g):
        origin = (y + NY - 1) % NY if g % 2 == 0 else (y + 1) % NY
        part = nb.at[origin, pl.ds(g * PER, PER)]
        return remote(part, part, S("yf_s").at[g], S("yf_r").at[g], (yup, ydn)[g % 2])

    def send_own(g):
        for i in range(g * PER, (g + 1) * PER):
            o = owner_s[i % NEIGH, i // NEIGH]
            rel = (o // PLANE - z + NZ) % NZ
            nb[y, i] = got[o % PLANE, jnp.where(rel < 8, 2 * rel, 31 - 2 * rel)]
        for way in range(2):
            copy = own_y(g, way)
            copy.start()
            sent.append(copy)

    ahead, behind = 4, 2
    for g in range(ahead):
        send_own(g)
    for s in (6, 7, 8):
        place_weights(s)
    for copy in loads:
        copy.wait()
    stores = []

    def attend(g):
        forward_y(g).wait_recv()
        attend_chunk(
            g, nb, weights, queries, grads, valid_s, attended, S("cot"), S("rows_t")
        )
        piece = pl.ds(g * 128, 128)
        copy = pltpu.make_async_copy(
            attended.at[piece], attended_h.at[piece], S("out_sem").at[g]
        )
        copy.start()
        stores.append(copy)

    for g in range(CHUNKS):
        for way in range(2):
            own_y(g, way).wait_recv()
        copy = forward_y(g)
        copy.start()
        sent.append(copy)
        if g + ahead < CHUNKS:
            send_own(g + ahead)
        if g >= behind:
            attend(g - behind)
    for g in range(CHUNKS - behind, CHUNKS):
        attend(g)

    for copy in sent:
        copy.wait_send()
    for copy in stores:
        copy.wait()
    rows_t, cot, total = S("rows_t"), S("cot"), S("total")
    c_send, c_recv, x_send, x_recv = map(S, ("c_send", "c_recv", "x_send", "x_recv"))
    own, z_send, z_recv = map(S, ("own", "z_send", "z_recv"))
    core_copies, x_copies, z_copies = [], [], []
    for h in range(2):
        theirs = pl.ds(pl.multiple_of((1 - c) * WIDTH + h * 256, 128), 256)
        c_send[h] = dot(rows_t[...], cot[:, theirs]).astype(BF16)
        copy = remote(c_send.at[h], c_recv.at[h], S("cs").at[h], S("cr").at[h], mate)
        copy.start()
        core_copies.append(copy)
    for h in range(2):
        mine = pl.ds(pl.multiple_of(c * WIDTH + h * 256, 128), 256)
        part = dot(rows_t[...], cot[:, mine])
        core_copies[h].wait_recv()
        total[h] = (part + c_recv[h].astype(F32)).reshape(NZ, NX, 8, 256)
        for t in range(1, NX):
            x_send[h, t - 1] = total[h, :, (x + t) % NX].reshape(128, 256).astype(BF16)
            copy = remote(
                x_send.at[h, t - 1],
                x_recv.at[h, t - 1],
                S("xs").at[h, t - 1],
                S("xr").at[h, t - 1],
                x_peer[t - 1],
            )
            copy.start()
            x_copies.append(copy)
    for h in range(2):
        line_sum = total[h, :, x]
        for t in range(1, NX):
            x_copies[h * 3 + t - 1].wait_recv()
            line_sum = line_sum + x_recv[h, t - 1].astype(F32).reshape(NZ, 8, 256)
        line_sum = jnp.concatenate([line_sum[:, :, :128], line_sum[:, :, 128:]], axis=1)
        own[h] = line_sum
        z_send[h] = line_sum.astype(BF16)
        for t in range(1, NZ):
            copy = remote(
                z_send.at[h, (z + t) % NZ],
                z_recv.at[h, t - 1],
                S("zs").at[h, t - 1],
                S("zr").at[h, t - 1],
                z_peer[t - 1],
            )
            copy.start()
            z_copies.append(copy)
    fin, fin_in = S("fin"), S("fin_in")
    for h in range(2):
        done = own[h, z]
        for t in range(1, NZ):
            z_copies[h * 15 + t - 1].wait_recv()
            done = done + z_recv[h, t - 1].astype(F32)
        fin[:, h * 256 : h * 256 + 128] = done[:8]
        fin[:, h * 256 + 128 : h * 256 + 256] = done[8:]
    last = remote(fin, fin_in, S("fs"), S("fr"), mate)
    last.start()
    for copy in core_copies + x_copies + z_copies:
        copy.wait_send()
    last.wait()
    even = c == 0
    sums = S("sums")
    sums[0] = jnp.where(even, fin[...], fin_in[...])
    sums[1] = jnp.where(even, fin_in[...], fin[...])
    copy = pltpu.make_async_copy(sums, sums_h, local_sem.at[4])
    copy.start()
    copy.wait()


def step(queries, out_grad, store, key_weight, value_weight, owner, row, valid):
    dma = pltpu.SemaphoreType.DMA
    scratch = {
        "tab_v": VM((PLANE, 1, 128), jnp.int32),
        "tab_s": pltpu.SMEM((PLANE, 1, 128), jnp.int32),
        "stage": VM((PLANE, 16, NB_LEN, 128), BF16),
        "got": VM((PLANE, 16, NB_LEN, 128), BF16),
        "wall": VM((PLANE, 16, 16, 256), BF16),
        "nb": VM((NY, SLOTS, NB_LEN, 128), BF16),
        "weights": VM((ENC_WIDTH, 2 * WIDTH), BF16),
        "queries": VM((BLOCKS * BLOCK_LEN, WIDTH), BF16),
        "grads": VM((BLOCKS * BLOCK_LEN, WIDTH), BF16),
        "attended": VM((BLOCKS * BLOCK_LEN, WIDTH), BF16),
        "cot": VM((ROWS, 2 * WIDTH), BF16),
        "rows_t": VM((ENC_WIDTH, ROWS), BF16),
        "c_send": VM((2, ENC_WIDTH, 256), BF16),
        "c_recv": VM((2, ENC_WIDTH, 256), BF16),
        "total": VM((2, NZ, NX, 8, 256), F32),
        "x_send": VM((2, NX - 1, 128, 256), BF16),
        "x_recv": VM((2, NX - 1, 128, 256), BF16),
        "own": VM((2, NZ, 16, 128), F32),
        "z_send": VM((2, NZ, 16, 128), BF16),
        "z_recv": VM((2, NZ - 1, 16, 128), BF16),
        "fin": VM((8, WIDTH), F32),
        "fin_in": VM((8, WIDTH), F32),
        "local_sem": dma((5,)),
        "store": VM((16, NB_LEN, 128), BF16),
        "sums": VM((2, 8, WIDTH), F32),
        "out_sem": dma((CHUNKS,)),
        "fs": dma,
        "fr": dma,
    }
    for send, recv, shape in (
        ("ring_s", "ring_r", (2, 8, 2)),
        ("wring_s", "wring_r", (2, 8)),
        ("cell_s", "cell_r", (PLANE, 9)),
        ("wc_s", "wc_r", (PLANE, 9)),
        ("tab_ss", "tab_rs", (PLANE,)),
        ("ys_s", "ys_r", (2, CHUNKS)),
        ("yf_s", "yf_r", (CHUNKS,)),
        ("cs", "cr", (2,)),
        ("xs", "xr", (2, NX - 1)),
        ("zs", "zr", (2, NZ - 1)),
    ):
        scratch[send] = dma(shape)
        scratch[recv] = dma(shape)
    anywhere = pl.BlockSpec(memory_space=pl.ANY)
    return pl.pallas_call(
        functools.partial(step_kernel, tuple(scratch)),
        out_shape=(
            jax.ShapeDtypeStruct((BLOCKS * BLOCK_LEN, WIDTH), BF16),
            jax.ShapeDtypeStruct((2, 8, WIDTH), F32),
        ),
        in_specs=[anywhere] + [VSPEC] * 2 + [SSPEC] * 3 + [anywhere] * 2,
        out_specs=(anywhere, anywhere),
        scratch_shapes=[VM((16, NB_LEN, 128), BF16)] * 15 + list(scratch.values()),
        compiler_params=pltpu.CompilerParams(
            collective_id=0, has_side_effects=True, vmem_limit_bytes=VLIMIT
        ),
    )(store, key_weight, value_weight, owner.T, row.T, valid.T, queries, out_grad)


def finish_kernel(attended_in, sums_in, attended, key_out, value_out, held, sums, key, value, sem_in, sem_out, sem):
    count = sem_in.shape[0]
    size = held.shape[0] // count
    pieces = [pl.ds(i * size, size) for i in range(count)]
    first = pltpu.make_async_copy(sums_in, sums, sem.at[0])
    first.start()
    inward = [
        pltpu.make_async_copy(attended_in.at[piece], held.at[piece], sem_in.at[i])
        for i, piece in enumerate(pieces)
    ]
    outward = [
        pltpu.make_async_copy(held.at[piece], attended.at[piece], sem_out.at[i])
        for i, piece in enumerate(pieces)
    ]
    outward += [
        pltpu.make_async_copy(key, key_out, sem.at[1]),
        pltpu.make_async_copy(value, value_out, sem.at[2]),
    ]
    for copy in inward:
        copy.start()
    low = lax.axis_index("dp") % 2 == 0
    first.wait()
    key[...] = jnp.where(low, sums[0, :4], sums[0, 4:])
    value[...] = jnp.where(low, sums[1, :4], sums[1, 4:])
    for copy in outward[count:]:
        copy.start()
    for i in range(count):
        inward[i].wait()
        outward[i].start()
    for copy in outward:
        copy.wait()


def finish(attended, sums):
    anywhere = pl.BlockSpec(memory_space=pl.ANY)
    dma = pltpu.SemaphoreType.DMA
    gradient = (4, WIDTH)
    return pl.pallas_call(
        finish_kernel,
        out_shape=(
            jax.ShapeDtypeStruct(attended.shape, BF16),
            jax.ShapeDtypeStruct(gradient, F32),
            jax.ShapeDtypeStruct(gradient, F32),
        ),
        in_specs=[anywhere] * 2,
        out_specs=(anywhere,) * 3,
        scratch_shapes=[
            VM(attended.shape, BF16),
            VM(sums.shape, F32),
            VM(gradient, F32),
            VM(gradient, F32),
            dma((CHUNKS,)),
            dma((CHUNKS,)),
            dma((3,)),
        ],
        compiler_params=pltpu.CompilerParams(vmem_limit_bytes=VLIMIT),
    )(attended, sums)


def shards(queries, out_grad, store, key_weight, value_weight, owner, row, valid):
    attended, sums = step(
        queries, out_grad, store, key_weight, value_weight, owner, row, valid
    )
    return finish(attended, sums)


def solution(mesh):
    in_specs = (
        P("dp", "mp"),
        P("dp", "mp"),
        P("dp", None, "mp"),
        P("dp", "mp"),
        P("dp", "mp"),
        P("dp", None),
        P("dp", None),
        P("dp", None),
    )
    out_specs = (P("dp", "mp"), P("dp", "mp"), P("dp", "mp"))
    return jax.shard_map(shards, mesh=mesh, in_specs=in_specs, out_specs=out_specs, check_vma=False)
```

```python
import functools
import math

import jax
import jax.numpy as jnp
from jax import lax
from jax.experimental import pallas as pl
from jax.experimental.pallas import tpu as pltpu
from jax.sharding import PartitionSpec as P

HEAD_DIM = 128
ENC_WIDTH = 512
BLOCK_LEN = 64
NEIGH = 2
NB_LEN = 64
BLOCKS = 14
SLOTS = BLOCKS * NEIGH
ROWS = SLOTS * NB_LEN
HEADS_DEV = 4
WIDTH = HEADS_DEV * HEAD_DIM
NZ, NX, NY, PLANE = 16, 4, 4, 8
CHUNKS = 7
FAR_FIRST = (4, 5, 2, 3, 6, 7, 1, 0)
PER = SLOTS // CHUNKS

MESH = pl.DeviceIdType.MESH
F32 = jnp.float32
BF16 = jnp.bfloat16
VM = pltpu.VMEM
VLIMIT = 56 * 2**20


def remote(src, dst, send, recv, device):
    return pltpu.make_async_remote_copy(
        src_ref=src,
        dst_ref=dst,
        send_sem=send,
        recv_sem=recv,
        device_id=device,
        device_id_type=MESH,
    )


def dot(a, b):
    return jnp.dot(a, b, preferred_element_type=F32)


def dot_t(a, b):
    return lax.dot_general(a, b, (((1,), (1,)), ((), ())), preferred_element_type=F32)


def attend_chunk(g, nb, weights, queries, grads, valid, attended, cot, rows_t):
    factor = 1.0 / math.sqrt(HEAD_DIM)
    rows = jnp.concatenate(
        [nb[f, g * PER : (g + 1) * PER].reshape(PER * NB_LEN, 128) for f in range(NY)], axis=1
    )
    states = dot(rows, weights[...]).astype(BF16)
    rows_t[:, g * 256 : (g + 1) * 256] = rows.T
    key_pos = lax.broadcasted_iota(jnp.int32, (NEIGH * NB_LEN, 2 * BLOCK_LEN), 0)
    zero = jnp.zeros((BLOCK_LEN, HEAD_DIM), BF16)

    def diagonal(ref, at, lane):
        return jnp.concatenate(
            [
                jnp.concatenate([ref[at, lane : lane + 128], zero], axis=1),
                jnp.concatenate([zero, ref[at, lane + 128 : lane + 256]], axis=1),
            ],
            axis=0,
        )

    for b in range(2):
        block = 2 * g + b
        first, second = valid[0, block], valid[1, block]
        allowed = (key_pos < first) | ((key_pos >= NB_LEN) & (key_pos < NB_LEN + second))
        at = slice(block * BLOCK_LEN, (block + 1) * BLOCK_LEN)
        to = slice(block * 128, block * 128 + 128)
        for lane in range(0, WIDTH, 256):
            key = states[b * 128 : b * 128 + 128, lane : lane + 256]
            value = states[b * 128 : b * 128 + 128, WIDTH + lane : WIDTH + lane + 256]
            query, grad = diagonal(queries, at, lane), diagonal(grads, at, lane)
            scores = jnp.where(allowed, factor * dot_t(key, query), -jnp.inf)
            exponent = jnp.exp(scores - jnp.max(scores, axis=0, keepdims=True))
            prob = exponent * (1.0 / jnp.sum(exponent, axis=0, keepdims=True))
            rounded = prob.astype(BF16)
            out = dot(rounded.T, value).astype(BF16)
            attended[at, lane : lane + 128] = out[:BLOCK_LEN, :128]
            attended[at, lane + 128 : lane + 256] = out[BLOCK_LEN:, 128:]
            grad_prob = dot_t(value, grad)
            inner = jnp.sum(prob * grad_prob, axis=0, keepdims=True)
            grad_score = (prob * (grad_prob - inner)).astype(BF16)
            cot[to, lane : lane + 256] = (factor * dot(grad_score, query)).astype(BF16)
            cot[to, WIDTH + lane : WIDTH + lane + 256] = dot(rounded, grad).astype(BF16)


def step_kernel(names, *refs):
    (store_h, kw_h, vw_h, owner_h, row_h, valid_h, queries_h, grads_h, attended_h, sums_h) = refs[:10]
    planes, named = refs[10:24], dict(zip(names, refs[24:]))
    S = named.__getitem__
    store, kw, vw = map(S, ("store", "kw", "vw"))
    owner_s, row_s, valid_s = map(S, ("owner_s", "row_s", "valid_s"))
    tab_v, tab_s, stage, got, wall = map(S, ("tab_v", "tab_s", "stage", "got", "wall"))
    nb, weights, queries, grads, attended = map(S, ("nb", "weights", "queries", "grads", "attended"))
    ups = [store] + [planes[2 * s - 2] for s in range(1, 8)]
    dns = [store] + [planes[2 * s - 1] for s in range(1, 8)]
    me = lax.axis_index("dp")
    y = lax.axis_index("mp")
    z, r = me // PLANE, me % PLANE
    x, c = r // 2, r % 2
    zup = (((z + 1) % NZ) * PLANE + r, y)
    zdn = (((z + NZ - 1) % NZ) * PLANE + r, y)
    peer = [(z * PLANE + (r + t) % PLANE, y) for t in range(PLANE)]
    yup, ydn = (me, (y + 1) % NY), (me, (y + NY - 1) % NY)
    mate = (me + 1 - 2 * c, y)
    x_peer = [(z * PLANE + ((x + t) % NX) * 2 + c, y) for t in range(1, NX)]
    z_peer = [(((z + t) % NZ) * PLANE + r, y) for t in range(1, NZ)]

    local_sem = S("local_sem")
    friends = [zup, zdn, yup, ydn] + peer[1:]
    barrier = pltpu.get_barrier_semaphore()
    for friend in friends:
        pl.semaphore_signal(barrier, inc=1, device_id=friend, device_id_type=MESH)
    early = [
        pltpu.make_async_copy(here, there, S("early_sem").at[i])
        for i, (here, there) in enumerate(
            (
                (store_h, store),
                (kw_h, kw),
                (vw_h, vw),
                (owner_h, owner_s),
                (row_h, row_s),
                (valid_h, valid_s),
            )
        )
    ]
    for copy in early:
        copy.start()
    loads = [
        pltpu.make_async_copy(queries_h, queries, local_sem.at[0]),
        pltpu.make_async_copy(grads_h, grads, local_sem.at[1]),
    ]
    for copy in loads:
        copy.start()
    pl.semaphore_wait(barrier, len(friends))
    for copy in early:
        copy.wait()

    lane = lax.broadcasted_iota(jnp.int32, (1, 128), 1)
    wanted = jnp.zeros((1, 128), jnp.int32)
    for j in range(NEIGH):
        for b in range(BLOCKS):
            wanted = wanted + jnp.where(lane == owner_s[j, b], row_s[j, b], 0)
    tab_v[r] = wanted
    both = jnp.concatenate([kw[...].astype(F32), vw[...].astype(F32)], axis=0)
    wall[r, 0] = jnp.concatenate([both[:, :256], both[:, 256:]], axis=0).astype(BF16)

    tab_copies = [
        remote(tab_v.at[r], tab_v.at[r], S("tab_ss").at[t], S("tab_rs").at[t], peer[t])
        for t in range(1, PLANE)
    ]
    for copy in tab_copies:
        copy.start()

    far_out, far_in = S("far_out"), S("far_in")
    tab_near = [
        remote(tab_v, S("near_v").at[way], S("near_ss").at[way], S("near_rs").at[way], (zup, zdn)[way])
        for way in range(2)
    ]

    def far_cells(way):
        half = pl.ds(way * 4, 4)
        return remote(
            far_out.at[half], far_in.at[half], S("far_s").at[way], S("far_r").at[way], (zup, zdn)[way]
        )

    def ring(s, way, part):
        bufs = (ups, dns)[way]
        piece = pl.ds(part * 8, 8)
        return remote(
            bufs[s].at[piece],
            bufs[s + 1].at[piece],
            S("ring_s").at[way, s, part],
            S("ring_r").at[way, s, part],
            (zup, zdn)[way],
        )

    def place(s, way):
        return 0 if s == 0 else 15 if s == 8 else 2 * s - 1 + way

    def cut_of(s):
        return pl.ds(place(s, 0), 1 if s in (0, 8) else 2)

    def weight_ring(s, way):
        return remote(
            wall.at[r, place(s, way)],
            wall.at[r, place(s + 1, way)],
            S("wring_s").at[way, s],
            S("wring_r").at[way, s],
            (zup, zdn)[way],
        )

    def weight_plane(s, t):
        rows = wall.at[r, cut_of(s)]
        return remote(rows, rows, S("wc_s").at[t, s], S("wc_r").at[t, s], peer[t])

    def cell_plane(s, t):
        return remote(
            far_in.at[pl.ds((r + t) % PLANE, 1)] if s == 8 else stage.at[t, cut_of(s)],
            got.at[r, cut_of(s)],
            S("cell_s").at[t, s],
            S("cell_r").at[t, s],
            peer[t],
        )

    line = lax.broadcasted_iota(jnp.int32, (64, 128), 0)
    column = lax.broadcasted_iota(jnp.int32, (64, 128), 1)
    line = (line % 32) // 4 * 16 + line // 32 * 4 + line % 4
    picks = [jnp.where(line + half * 8 == column, 1.0, 0.0).astype(BF16) for half in range(2)]

    def place_weights(s):
        for t in range(1, PLANE):
            weight_plane(s, t).wait_recv()
        for way in range(1 if s in (0, 8) else 2):
            far = (z + NZ - s) % NZ if way == 0 else (z + s) % NZ
            tiles = wall[:, place(s, way)].reshape(128, 256)
            at = pl.ds(pl.multiple_of(far * 32, 32), 32)
            for half in range(2):
                ordered = dot(picks[half], tiles).astype(BF16)
                weights[at, half * 256 : half * 256 + 256] = ordered[:32]
                weights[at, WIDTH + half * 256 : WIDTH + half * 256 + 256] = ordered[32:]

    sent = []
    for s in range(9):
        if s > 0:
            for way in (0,) if s == 8 else (0, 1):
                weight_ring(s - 1, way).wait_recv()
        if s < 8:
            for way in (0,) if s == 7 else (0, 1):
                copy = weight_ring(s, way)
                copy.start()
                sent.append(copy)
        for part in range(2):
            for way in range(2):
                if 0 < s < 8:
                    ring(s - 1, way, part).wait_recv()
                if s < 7:
                    copy = ring(s, way, part)
                    copy.start()
                    sent.append(copy)
        if s == 0:
            for copy in tab_copies:
                copy.wait()
            local = pltpu.make_async_copy(tab_v, tab_s, local_sem.at[2])
            local.start()
            local.wait()
            for copy in tab_near:
                copy.start()
                sent.append(copy)
        if s == 1:
            for copy in tab_near:
                copy.wait_recv()
            local = pltpu.make_async_copy(S("near_v"), S("near_s"), local_sem.at[3])
            local.start()
            local.wait()
        if s == 7:
            for way in range(2):
                buf = (ups, dns)[way][7]
                far = (z + NZ - 7) % NZ if way == 0 else (z + 7) % NZ
                for i in range(way * 4, way * 4 + 4):
                    far_out[i] = buf[S("near_s")[1 - way, i, 0, far * PLANE + r]]
                copy = far_cells(way)
                copy.start()
                sent.append(copy)
        if s == 8:
            for way in range(2):
                far_cells(way).wait_recv()
            got[r, 15] = far_in[r]
        for t in FAR_FIRST:
            for way in range((2, 1)[s == 0] if s < 8 else 0):
                buf = (ups, dns)[way][s]
                far = (z + NZ - s) % NZ if way == 0 else (z + s) % NZ
                entry = buf[tab_s[(r + t) % PLANE, 0, far * PLANE + r]]
                if t == 0:
                    got[r, place(s, way)] = entry
                else:
                    stage[t, place(s, way)] = entry
            if t > 0:
                copy = cell_plane(s, t)
                copy.start()
                sent.append(copy)
        for late in () if s == 0 else (s - 1,) if s < 8 else (7, 8):
            for t in range(1, PLANE):
                copy = weight_plane(late, t)
                copy.start()
                sent.append(copy)
        if s >= 3:
            place_weights(s - 3)
    for s in range(9):
        for t in range(1, PLANE):
            cell_plane(s, t).wait_recv()

    def own_y(g, way):
        part = nb.at[y, pl.ds(g * PER, PER)]
        return remote(part, part, S("ys_s").at[way, g], S("ys_r").at[way, g], (yup, ydn)[way])

    def forward_y(g, way):
        origin = (y + NY - 1) % NY if way == 0 else (y + 1) % NY
        half = PER // 2
        part = nb.at[origin, pl.ds(g * PER + way * half, half)]
        return remote(part, part, S("yf_s").at[way, g], S("yf_r").at[way, g], (yup, ydn)[way])

    def send_own(g):
        for i in range(g * PER, (g + 1) * PER):
            o = owner_s[i % NEIGH, i // NEIGH]
            rel = (o // PLANE - z + NZ) % NZ
            nb[y, i] = got[o % PLANE, jnp.where(rel < 8, 2 * rel, 31 - 2 * rel)]
        for way in range(2):
            copy = own_y(g, way)
            copy.start()
            sent.append(copy)

    ahead, behind = 3, 2
    for g in range(ahead):
        send_own(g)
    for s in (6, 7, 8):
        place_weights(s)
    for copy in loads:
        copy.wait()
    stores = []

    def attend(g):
        for way in range(2):
            forward_y(g, way).wait_recv()
        attend_chunk(
            g, nb, weights, queries, grads, valid_s, attended, S("cot"), S("rows_t")
        )
        piece = pl.ds(g * 128, 128)
        copy = pltpu.make_async_copy(
            attended.at[piece], attended_h.at[piece], S("out_sem").at[g]
        )
        copy.start()
        stores.append(copy)

    for g in range(CHUNKS):
        for way in range(2):
            own_y(g, way).wait_recv()
            copy = forward_y(g, way)
            copy.start()
            sent.append(copy)
        if g + ahead < CHUNKS:
            send_own(g + ahead)
        if g >= behind:
            attend(g - behind)
    for g in range(CHUNKS - behind, CHUNKS):
        attend(g)

    for copy in sent:
        copy.wait_send()
    for copy in stores:
        copy.wait()
    rows_t, cot, total = S("rows_t"), S("cot"), S("total")
    c_send, c_recv, x_send, x_recv = map(S, ("c_send", "c_recv", "x_send", "x_recv"))
    own, z_send, z_recv = map(S, ("own", "z_send", "z_recv"))
    core_copies, x_copies, z_copies = [], [], []
    for h in range(2):
        theirs = pl.ds(pl.multiple_of((1 - c) * WIDTH + h * 256, 128), 256)
        c_send[h] = dot(rows_t[...], cot[:, theirs]).astype(BF16)
        copy = remote(c_send.at[h], c_recv.at[h], S("cs").at[h], S("cr").at[h], mate)
        copy.start()
        core_copies.append(copy)
    for h in range(2):
        mine = pl.ds(pl.multiple_of(c * WIDTH + h * 256, 128), 256)
        part = dot(rows_t[...], cot[:, mine])
        core_copies[h].wait_recv()
        total[h] = (part + c_recv[h].astype(F32)).reshape(NZ, NX, 8, 256)
        for t in range(1, NX):
            x_send[h, t - 1] = total[h, :, (x + t) % NX].reshape(128, 256).astype(BF16)
            copy = remote(
                x_send.at[h, t - 1],
                x_recv.at[h, t - 1],
                S("xs").at[h, t - 1],
                S("xr").at[h, t - 1],
                x_peer[t - 1],
            )
            copy.start()
            x_copies.append(copy)
    for h in range(2):
        line_sum = total[h, :, x]
        for t in range(1, NX):
            x_copies[h * 3 + t - 1].wait_recv()
            line_sum = line_sum + x_recv[h, t - 1].astype(F32).reshape(NZ, 8, 256)
        line_sum = jnp.concatenate([line_sum[:, :, :128], line_sum[:, :, 128:]], axis=1)
        own[h] = line_sum
        z_send[h] = line_sum.astype(BF16)
        for t in range(1, NZ):
            copy = remote(
                z_send.at[h, (z + t) % NZ],
                z_recv.at[h, t - 1],
                S("zs").at[h, t - 1],
                S("zr").at[h, t - 1],
                z_peer[t - 1],
            )
            copy.start()
            z_copies.append(copy)
    fin, fin_in = S("fin"), S("fin_in")
    for h in range(2):
        done = own[h, z]
        for t in range(1, NZ):
            z_copies[h * 15 + t - 1].wait_recv()
            done = done + z_recv[h, t - 1].astype(F32)
        fin[:, h * 256 : h * 256 + 128] = done[:8]
        fin[:, h * 256 + 128 : h * 256 + 256] = done[8:]
    last = remote(fin, fin_in, S("fs"), S("fr"), mate)
    last.start()
    for copy in core_copies + x_copies + z_copies:
        copy.wait_send()
    last.wait()
    even = c == 0
    sums = S("sums")
    sums[0] = jnp.where(even, fin[...], fin_in[...])
    sums[1] = jnp.where(even, fin_in[...], fin[...])
    copy = pltpu.make_async_copy(sums, sums_h, local_sem.at[4])
    copy.start()
    copy.wait()


def step(queries, out_grad, store, key_weight, value_weight, owner, row, valid):
    dma = pltpu.SemaphoreType.DMA
    scratch = {
        "tab_v": VM((PLANE, 1, 128), jnp.int32),
        "tab_s": pltpu.SMEM((PLANE, 1, 128), jnp.int32),
        "stage": VM((PLANE, 16, NB_LEN, 128), BF16),
        "got": VM((PLANE, 16, NB_LEN, 128), BF16),
        "wall": VM((PLANE, 16, 16, 256), BF16),
        "nb": VM((NY, SLOTS, NB_LEN, 128), BF16),
        "weights": VM((ENC_WIDTH, 2 * WIDTH), BF16),
        "queries": VM((BLOCKS * BLOCK_LEN, WIDTH), BF16),
        "grads": VM((BLOCKS * BLOCK_LEN, WIDTH), BF16),
        "attended": VM((BLOCKS * BLOCK_LEN, WIDTH), BF16),
        "cot": VM((ROWS, 2 * WIDTH), BF16),
        "rows_t": VM((ENC_WIDTH, ROWS), BF16),
        "c_send": VM((2, ENC_WIDTH, 256), BF16),
        "c_recv": VM((2, ENC_WIDTH, 256), BF16),
        "total": VM((2, NZ, NX, 8, 256), F32),
        "x_send": VM((2, NX - 1, 128, 256), BF16),
        "x_recv": VM((2, NX - 1, 128, 256), BF16),
        "own": VM((2, NZ, 16, 128), F32),
        "z_send": VM((2, NZ, 16, 128), BF16),
        "z_recv": VM((2, NZ - 1, 16, 128), BF16),
        "fin": VM((8, WIDTH), F32),
        "fin_in": VM((8, WIDTH), F32),
        "local_sem": dma((5,)),
        "near_v": VM((2, PLANE, 1, 128), jnp.int32),
        "near_s": pltpu.SMEM((2, PLANE, 1, 128), jnp.int32),
        "far_out": VM((PLANE, NB_LEN, 128), BF16),
        "far_in": VM((PLANE, NB_LEN, 128), BF16),
        "early_sem": dma((6,)),
        "kw": VM((4, WIDTH), BF16),
        "vw": VM((4, WIDTH), BF16),
        "owner_s": pltpu.SMEM((NEIGH, BLOCKS), jnp.int32),
        "row_s": pltpu.SMEM((NEIGH, BLOCKS), jnp.int32),
        "valid_s": pltpu.SMEM((NEIGH, BLOCKS), jnp.int32),
        "store": VM((16, NB_LEN, 128), BF16),
        "sums": VM((2, 8, WIDTH), F32),
        "out_sem": dma((CHUNKS,)),
        "fs": dma,
        "fr": dma,
    }
    for send, recv, shape in (
        ("ring_s", "ring_r", (2, 7, 2)),
        ("near_ss", "near_rs", (2,)),
        ("far_s", "far_r", (2,)),
        ("wring_s", "wring_r", (2, 8)),
        ("cell_s", "cell_r", (PLANE, 9)),
        ("wc_s", "wc_r", (PLANE, 9)),
        ("tab_ss", "tab_rs", (PLANE,)),
        ("ys_s", "ys_r", (2, CHUNKS)),
        ("yf_s", "yf_r", (2, CHUNKS)),
        ("cs", "cr", (2,)),
        ("xs", "xr", (2, NX - 1)),
        ("zs", "zr", (2, NZ - 1)),
    ):
        scratch[send] = dma(shape)
        scratch[recv] = dma(shape)
    anywhere = pl.BlockSpec(memory_space=pl.ANY)
    return pl.pallas_call(
        functools.partial(step_kernel, tuple(scratch)),
        out_shape=(
            jax.ShapeDtypeStruct((BLOCKS * BLOCK_LEN, WIDTH), BF16),
            jax.ShapeDtypeStruct((2, 8, WIDTH), F32),
        ),
        in_specs=[anywhere] * 8,
        out_specs=(anywhere, anywhere),
        scratch_shapes=[VM((16, NB_LEN, 128), BF16)] * 14 + list(scratch.values()),
        compiler_params=pltpu.CompilerParams(
            collective_id=0, has_side_effects=True, vmem_limit_bytes=VLIMIT
        ),
    )(store, key_weight, value_weight, owner.T, row.T, valid.T, queries, out_grad)


def finish_kernel(attended_in, sums_in, attended, key_out, value_out, held, sums, key, value, sem_in, sem_out, sem):
    count = sem_in.shape[0]
    size = held.shape[0] // count
    pieces = [pl.ds(i * size, size) for i in range(count)]
    first = pltpu.make_async_copy(sums_in, sums, sem.at[0])
    first.start()
    inward = [
        pltpu.make_async_copy(attended_in.at[piece], held.at[piece], sem_in.at[i])
        for i, piece in enumerate(pieces)
    ]
    outward = [
        pltpu.make_async_copy(held.at[piece], attended.at[piece], sem_out.at[i])
        for i, piece in enumerate(pieces)
    ]
    outward += [
        pltpu.make_async_copy(key, key_out, sem.at[1]),
        pltpu.make_async_copy(value, value_out, sem.at[2]),
    ]
    for copy in inward:
        copy.start()
    low = lax.axis_index("dp") % 2 == 0
    first.wait()
    key[...] = jnp.where(low, sums[0, :4], sums[0, 4:])
    value[...] = jnp.where(low, sums[1, :4], sums[1, 4:])
    for copy in outward[count:]:
        copy.start()
    for i in range(count):
        inward[i].wait()
        outward[i].start()
    for copy in outward:
        copy.wait()


def finish(attended, sums):
    anywhere = pl.BlockSpec(memory_space=pl.ANY)
    dma = pltpu.SemaphoreType.DMA
    gradient = (4, WIDTH)
    return pl.pallas_call(
        finish_kernel,
        out_shape=(
            jax.ShapeDtypeStruct(attended.shape, BF16),
            jax.ShapeDtypeStruct(gradient, F32),
            jax.ShapeDtypeStruct(gradient, F32),
        ),
        in_specs=[anywhere] * 2,
        out_specs=(anywhere,) * 3,
        scratch_shapes=[
            VM(attended.shape, BF16),
            VM(sums.shape, F32),
            VM(gradient, F32),
            VM(gradient, F32),
            dma((CHUNKS,)),
            dma((CHUNKS,)),
            dma((3,)),
        ],
        compiler_params=pltpu.CompilerParams(vmem_limit_bytes=VLIMIT),
    )(attended, sums)


def shards(queries, out_grad, store, key_weight, value_weight, owner, row, valid):
    attended, sums = step(
        queries, out_grad, store, key_weight, value_weight, owner, row, valid
    )
    return finish(attended, sums)


def solution(mesh):
    in_specs = (
        P("dp", "mp"),
        P("dp", "mp"),
        P("dp", None, "mp"),
        P("dp", "mp"),
        P("dp", "mp"),
        P("dp", None),
        P("dp", None),
        P("dp", None),
    )
    out_specs = (P("dp", "mp"), P("dp", "mp"), P("dp", "mp"))
    return jax.shard_map(shards, mesh=mesh, in_specs=in_specs, out_specs=out_specs, check_vma=False)
```

```python
import functools
import math

import jax
import jax.numpy as jnp
from jax import lax
from jax.experimental import pallas as pl
from jax.experimental.pallas import tpu as pltpu
from jax.sharding import PartitionSpec as P

HEAD_DIM = 128
ENC_WIDTH = 512
BLOCK_LEN = 64
NEIGH = 2
NB_LEN = 64
BLOCKS = 14
SLOTS = BLOCKS * NEIGH
ROWS = SLOTS * NB_LEN
HEADS_DEV = 4
WIDTH = HEADS_DEV * HEAD_DIM
NZ, NX, NY, PLANE = 16, 4, 4, 8
CHUNKS = 7
FAR_FIRST = (4, 5, 2, 3, 6, 7, 1, 0)
PER = SLOTS // CHUNKS

MESH = pl.DeviceIdType.MESH
F32 = jnp.float32
BF16 = jnp.bfloat16
VM = pltpu.VMEM
VLIMIT = 56 * 2**20


def remote(src, dst, send, recv, device):
    return pltpu.make_async_remote_copy(
        src_ref=src,
        dst_ref=dst,
        send_sem=send,
        recv_sem=recv,
        device_id=device,
        device_id_type=MESH,
    )


def dot(a, b):
    return jnp.dot(a, b, preferred_element_type=F32)


def dot_t(a, b):
    return lax.dot_general(a, b, (((1,), (1,)), ((), ())), preferred_element_type=F32)


def attend_chunk(g, nb, weights, queries, grads, valid, attended, cot, rows_t):
    factor = 1.0 / math.sqrt(HEAD_DIM)
    rows = jnp.concatenate(
        [nb[f, g * PER : (g + 1) * PER].reshape(PER * NB_LEN, 128) for f in range(NY)], axis=1
    )
    states = dot(rows, weights[...]).astype(BF16)
    rows_t[:, g * 256 : (g + 1) * 256] = rows.T
    key_pos = lax.broadcasted_iota(jnp.int32, (NEIGH * NB_LEN, 2 * BLOCK_LEN), 0)
    zero = jnp.zeros((BLOCK_LEN, HEAD_DIM), BF16)

    def diagonal(ref, at, lane):
        return jnp.concatenate(
            [
                jnp.concatenate([ref[at, lane : lane + 128], zero], axis=1),
                jnp.concatenate([zero, ref[at, lane + 128 : lane + 256]], axis=1),
            ],
            axis=0,
        )

    for b in range(2):
        block = 2 * g + b
        first, second = valid[0, block], valid[1, block]
        allowed = (key_pos < first) | ((key_pos >= NB_LEN) & (key_pos < NB_LEN + second))
        at = slice(block * BLOCK_LEN, (block + 1) * BLOCK_LEN)
        to = slice(block * 128, block * 128 + 128)
        for lane in range(0, WIDTH, 256):
            key = states[b * 128 : b * 128 + 128, lane : lane + 256]
            value = states[b * 128 : b * 128 + 128, WIDTH + lane : WIDTH + lane + 256]
            query, grad = diagonal(queries, at, lane), diagonal(grads, at, lane)
            scores = jnp.where(allowed, factor * dot_t(key, query), -jnp.inf)
            exponent = jnp.exp(scores - jnp.max(scores, axis=0, keepdims=True))
            prob = exponent * (1.0 / jnp.sum(exponent, axis=0, keepdims=True))
            rounded = prob.astype(BF16)
            out = dot(rounded.T, value).astype(BF16)
            attended[at, lane : lane + 128] = out[:BLOCK_LEN, :128]
            attended[at, lane + 128 : lane + 256] = out[BLOCK_LEN:, 128:]
            grad_prob = dot_t(value, grad)
            inner = jnp.sum(prob * grad_prob, axis=0, keepdims=True)
            grad_score = (prob * (grad_prob - inner)).astype(BF16)
            cot[to, lane : lane + 256] = (factor * dot(grad_score, query)).astype(BF16)
            cot[to, WIDTH + lane : WIDTH + lane + 256] = dot(rounded, grad).astype(BF16)


def step_kernel(names, *refs):
    (store_h, kw_h, vw_h, owner_h, row_h, valid_h, queries_h, grads_h, attended_h, sums_h) = refs[:10]
    planes, named = refs[10:24], dict(zip(names, refs[24:]))
    S = named.__getitem__
    store, kw, vw = map(S, ("store", "kw", "vw"))
    owner_s, row_s, valid_s = map(S, ("owner_s", "row_s", "valid_s"))
    tab_v, tab_s, stage, got, wall = map(S, ("tab_v", "tab_s", "stage", "got", "wall"))
    nb, weights, queries, grads, attended = map(S, ("nb", "weights", "queries", "grads", "attended"))
    ups = [store] + [planes[2 * s - 2] for s in range(1, 8)]
    dns = [store] + [planes[2 * s - 1] for s in range(1, 8)]
    me = lax.axis_index("dp")
    y = lax.axis_index("mp")
    z, r = me // PLANE, me % PLANE
    x, c = r // 2, r % 2
    zup = (((z + 1) % NZ) * PLANE + r, y)
    zdn = (((z + NZ - 1) % NZ) * PLANE + r, y)
    peer = [(z * PLANE + (r + t) % PLANE, y) for t in range(PLANE)]
    yup, ydn = (me, (y + 1) % NY), (me, (y + NY - 1) % NY)
    mate = (me + 1 - 2 * c, y)
    x_peer = [(z * PLANE + ((x + t) % NX) * 2 + c, y) for t in range(1, NX)]
    z_peer = [(((z + t) % NZ) * PLANE + r, y) for t in range(1, NZ)]

    local_sem = S("local_sem")
    friends = [zup, zdn, yup, ydn] + peer[1:]
    barrier = pltpu.get_barrier_semaphore()
    for friend in friends:
        pl.semaphore_signal(barrier, inc=1, device_id=friend, device_id_type=MESH)
    early = [
        pltpu.make_async_copy(here, there, S("early_sem").at[i])
        for i, (here, there) in enumerate(
            (
                (store_h, store),
                (kw_h, kw),
                (vw_h, vw),
                (owner_h, owner_s),
                (row_h, row_s),
                (valid_h, valid_s),
            )
        )
    ]
    for copy in early:
        copy.start()
    loads = [
        pltpu.make_async_copy(queries_h, queries, local_sem.at[0]),
        pltpu.make_async_copy(grads_h, grads, local_sem.at[1]),
    ]
    for copy in loads:
        copy.start()
    pl.semaphore_wait(barrier, len(friends))
    for copy in early:
        copy.wait()

    lane = lax.broadcasted_iota(jnp.int32, (1, 128), 1)
    wanted = jnp.zeros((1, 128), jnp.int32)
    for j in range(NEIGH):
        for b in range(BLOCKS):
            wanted = wanted + jnp.where(lane == owner_s[j, b], row_s[j, b], 0)
    tab_v[r] = wanted
    both = jnp.concatenate([kw[...].astype(F32), vw[...].astype(F32)], axis=0)
    wall[r, 0] = jnp.concatenate([both[:, :256], both[:, 256:]], axis=0).astype(BF16)

    tab_copies = [
        remote(tab_v.at[r], tab_v.at[r], S("tab_ss").at[t], S("tab_rs").at[t], peer[t])
        for t in range(1, PLANE)
    ]
    for copy in tab_copies:
        copy.start()

    far_out, far_in = S("far_out"), S("far_in")
    tab_near = [
        remote(tab_v, S("near_v").at[way], S("near_ss").at[way], S("near_rs").at[way], (zup, zdn)[way])
        for way in range(2)
    ]

    def far_cells(way):
        half = pl.ds(way * 4, 4)
        return remote(
            far_out.at[half], far_in.at[half], S("far_s").at[way], S("far_r").at[way], (zup, zdn)[way]
        )

    def ring(s, way, part):
        bufs = (ups, dns)[way]
        piece = pl.ds(part * 8, 8)
        return remote(
            bufs[s].at[piece],
            bufs[s + 1].at[piece],
            S("ring_s").at[way, s, part],
            S("ring_r").at[way, s, part],
            (zup, zdn)[way],
        )

    def place(s, way):
        return 0 if s == 0 else 15 if s == 8 else 2 * s - 1 + way

    def cut_of(s):
        return pl.ds(place(s, 0), 1 if s in (0, 8) else 2)

    def weight_ring(s, way):
        return remote(
            wall.at[r, place(s, way)],
            wall.at[r, place(s + 1, way)],
            S("wring_s").at[way, s],
            S("wring_r").at[way, s],
            (zup, zdn)[way],
        )

    def weight_plane(s, t):
        rows = wall.at[r, cut_of(s)]
        return remote(rows, rows, S("wc_s").at[t, s], S("wc_r").at[t, s], peer[t])

    def cell_plane(s, t):
        return remote(
            far_in.at[pl.ds((r + t) % PLANE, 1)] if s == 8 else stage.at[t, cut_of(s)],
            got.at[r, cut_of(s)],
            S("cell_s").at[t, s],
            S("cell_r").at[t, s],
            peer[t],
        )

    line = lax.broadcasted_iota(jnp.int32, (64, 128), 0)
    column = lax.broadcasted_iota(jnp.int32, (64, 128), 1)
    line = (line % 32) // 4 * 16 + line // 32 * 4 + line % 4
    picks = [jnp.where(line + half * 8 == column, 1.0, 0.0).astype(BF16) for half in range(2)]

    def place_weights(s):
        for t in range(1, PLANE):
            weight_plane(s, t).wait_recv()
        for way in range(1 if s in (0, 8) else 2):
            far = (z + NZ - s) % NZ if way == 0 else (z + s) % NZ
            tiles = wall[:, place(s, way)].reshape(128, 256)
            at = pl.ds(pl.multiple_of(far * 32, 32), 32)
            for half in range(2):
                ordered = dot(picks[half], tiles).astype(BF16)
                weights[at, half * 256 : half * 256 + 256] = ordered[:32]
                weights[at, WIDTH + half * 256 : WIDTH + half * 256 + 256] = ordered[32:]

    sent = []
    for s in range(9):
        if s > 0:
            for way in (0,) if s == 8 else (0, 1):
                weight_ring(s - 1, way).wait_recv()
        if s < 8:
            for way in (0,) if s == 7 else (0, 1):
                copy = weight_ring(s, way)
                copy.start()
                sent.append(copy)
        for part in range(2):
            for way in range(2):
                if 0 < s < 8:
                    ring(s - 1, way, part).wait_recv()
                if s < 7:
                    copy = ring(s, way, part)
                    copy.start()
                    sent.append(copy)
        if s == 0:
            for copy in tab_copies:
                copy.wait()
            local = pltpu.make_async_copy(tab_v, tab_s, local_sem.at[2])
            local.start()
            local.wait()
            for copy in tab_near:
                copy.start()
                sent.append(copy)
        if s == 1:
            for copy in tab_near:
                copy.wait_recv()
            local = pltpu.make_async_copy(S("near_v"), S("near_s"), local_sem.at[3])
            local.start()
            local.wait()
        if s == 7:
            for way in range(2):
                buf = (ups, dns)[way][7]
                far = (z + NZ - 7) % NZ if way == 0 else (z + 7) % NZ
                for i in range(way * 4, way * 4 + 4):
                    far_out[i] = buf[S("near_s")[1 - way, i, 0, far * PLANE + r]]
                copy = far_cells(way)
                copy.start()
                sent.append(copy)
        if s == 8:
            for way in range(2):
                far_cells(way).wait_recv()
            got[r, 15] = far_in[r]
        for t in FAR_FIRST:
            for way in range((2, 1)[s == 0] if s < 8 else 0):
                buf = (ups, dns)[way][s]
                far = (z + NZ - s) % NZ if way == 0 else (z + s) % NZ
                entry = buf[tab_s[(r + t) % PLANE, 0, far * PLANE + r]]
                if t == 0:
                    got[r, place(s, way)] = entry
                else:
                    stage[t, place(s, way)] = entry
            if t > 0:
                copy = cell_plane(s, t)
                copy.start()
                sent.append(copy)
        for late in () if s in (0, 7) else (s - 1,) if s < 8 else (6, 7, 8):
            for t in range(1, PLANE):
                copy = weight_plane(late, t)
                copy.start()
                sent.append(copy)
        if s >= 3:
            place_weights(s - 3)
    for s in range(9):
        for t in range(1, PLANE):
            cell_plane(s, t).wait_recv()

    def own_y(g, way):
        part = nb.at[y, pl.ds(g * PER, PER)]
        return remote(part, part, S("ys_s").at[way, g], S("ys_r").at[way, g], (yup, ydn)[way])

    def forward_y(g, way):
        origin = (y + NY - 1) % NY if way == 0 else (y + 1) % NY
        half = PER // 2
        part = nb.at[origin, pl.ds(g * PER + way * half, half)]
        return remote(part, part, S("yf_s").at[way, g], S("yf_r").at[way, g], (yup, ydn)[way])

    def send_own(g):
        for i in range(g * PER, (g + 1) * PER):
            o = owner_s[i % NEIGH, i // NEIGH]
            rel = (o // PLANE - z + NZ) % NZ
            nb[y, i] = got[o % PLANE, jnp.where(rel < 8, 2 * rel, 31 - 2 * rel)]
        for way in range(2):
            copy = own_y(g, way)
            copy.start()
            sent.append(copy)

    ahead, behind = 3, 2
    for g in range(ahead):
        send_own(g)
    stores = []

    def attend(g):
        for way in range(2):
            forward_y(g, way).wait_recv()
        attend_chunk(
            g, nb, weights, queries, grads, valid_s, attended, S("cot"), S("rows_t")
        )
        piece = pl.ds(g * 128, 128)
        copy = pltpu.make_async_copy(
            attended.at[piece], attended_h.at[piece], S("out_sem").at[g]
        )
        copy.start()
        stores.append(copy)

    for g in range(CHUNKS):
        for way in range(2):
            own_y(g, way).wait_recv()
            copy = forward_y(g, way)
            copy.start()
            sent.append(copy)
        if g + ahead < CHUNKS:
            send_own(g + ahead)
        if g == behind:
            for s in (6, 7, 8):
                place_weights(s)
            for copy in loads:
                copy.wait()
        if g >= behind:
            attend(g - behind)
    for g in range(CHUNKS - behind, CHUNKS):
        attend(g)

    for copy in sent:
        copy.wait_send()
    for copy in stores:
        copy.wait()
    rows_t, cot, total = S("rows_t"), S("cot"), S("total")
    c_send, c_recv, x_send, x_recv = map(S, ("c_send", "c_recv", "x_send", "x_recv"))
    own, z_send, z_recv = map(S, ("own", "z_send", "z_recv"))
    core_copies, x_copies, z_copies = [], [], []
    for h in range(2):
        theirs = pl.ds(pl.multiple_of((1 - c) * WIDTH + h * 256, 128), 256)
        c_send[h] = dot(rows_t[...], cot[:, theirs]).astype(BF16)
        copy = remote(c_send.at[h], c_recv.at[h], S("cs").at[h], S("cr").at[h], mate)
        copy.start()
        core_copies.append(copy)
    for h in range(2):
        mine = pl.ds(pl.multiple_of(c * WIDTH + h * 256, 128), 256)
        part = dot(rows_t[...], cot[:, mine])
        core_copies[h].wait_recv()
        total[h] = (part + c_recv[h].astype(F32)).reshape(NZ, NX, 8, 256)
        for t in range(1, NX):
            x_send[h, t - 1] = total[h, :, (x + t) % NX].reshape(128, 256).astype(BF16)
            copy = remote(
                x_send.at[h, t - 1],
                x_recv.at[h, t - 1],
                S("xs").at[h, t - 1],
                S("xr").at[h, t - 1],
                x_peer[t - 1],
            )
            copy.start()
            x_copies.append(copy)
    for h in range(2):
        line_sum = total[h, :, x]
        for t in range(1, NX):
            x_copies[h * 3 + t - 1].wait_recv()
            line_sum = line_sum + x_recv[h, t - 1].astype(F32).reshape(NZ, 8, 256)
        line_sum = jnp.concatenate([line_sum[:, :, :128], line_sum[:, :, 128:]], axis=1)
        own[h] = line_sum
        z_send[h] = line_sum.astype(BF16)
        for t in range(1, NZ):
            copy = remote(
                z_send.at[h, (z + t) % NZ],
                z_recv.at[h, t - 1],
                S("zs").at[h, t - 1],
                S("zr").at[h, t - 1],
                z_peer[t - 1],
            )
            copy.start()
            z_copies.append(copy)
    fin, fin_in = S("fin"), S("fin_in")
    for h in range(2):
        done = own[h, z]
        for t in range(1, NZ):
            z_copies[h * 15 + t - 1].wait_recv()
            done = done + z_recv[h, t - 1].astype(F32)
        fin[:, h * 256 : h * 256 + 128] = done[:8]
        fin[:, h * 256 + 128 : h * 256 + 256] = done[8:]
    last = remote(fin, fin_in, S("fs"), S("fr"), mate)
    last.start()
    for copy in core_copies + x_copies + z_copies:
        copy.wait_send()
    last.wait()
    even = c == 0
    sums = S("sums")
    sums[0] = jnp.where(even, fin[...], fin_in[...])
    sums[1] = jnp.where(even, fin_in[...], fin[...])
    copy = pltpu.make_async_copy(sums, sums_h, local_sem.at[4])
    copy.start()
    copy.wait()


def step(queries, out_grad, store, key_weight, value_weight, owner, row, valid):
    dma = pltpu.SemaphoreType.DMA
    scratch = {
        "tab_v": VM((PLANE, 1, 128), jnp.int32),
        "tab_s": pltpu.SMEM((PLANE, 1, 128), jnp.int32),
        "stage": VM((PLANE, 16, NB_LEN, 128), BF16),
        "got": VM((PLANE, 16, NB_LEN, 128), BF16),
        "wall": VM((PLANE, 16, 16, 256), BF16),
        "nb": VM((NY, SLOTS, NB_LEN, 128), BF16),
        "weights": VM((ENC_WIDTH, 2 * WIDTH), BF16),
        "queries": VM((BLOCKS * BLOCK_LEN, WIDTH), BF16),
        "grads": VM((BLOCKS * BLOCK_LEN, WIDTH), BF16),
        "attended": VM((BLOCKS * BLOCK_LEN, WIDTH), BF16),
        "cot": VM((ROWS, 2 * WIDTH), BF16),
        "rows_t": VM((ENC_WIDTH, ROWS), BF16),
        "c_send": VM((2, ENC_WIDTH, 256), BF16),
        "c_recv": VM((2, ENC_WIDTH, 256), BF16),
        "total": VM((2, NZ, NX, 8, 256), F32),
        "x_send": VM((2, NX - 1, 128, 256), BF16),
        "x_recv": VM((2, NX - 1, 128, 256), BF16),
        "own": VM((2, NZ, 16, 128), F32),
        "z_send": VM((2, NZ, 16, 128), BF16),
        "z_recv": VM((2, NZ - 1, 16, 128), BF16),
        "fin": VM((8, WIDTH), F32),
        "fin_in": VM((8, WIDTH), F32),
        "local_sem": dma((5,)),
        "near_v": VM((2, PLANE, 1, 128), jnp.int32),
        "near_s": pltpu.SMEM((2, PLANE, 1, 128), jnp.int32),
        "far_out": VM((PLANE, NB_LEN, 128), BF16),
        "far_in": VM((PLANE, NB_LEN, 128), BF16),
        "early_sem": dma((6,)),
        "kw": VM((4, WIDTH), BF16),
        "vw": VM((4, WIDTH), BF16),
        "owner_s": pltpu.SMEM((NEIGH, BLOCKS), jnp.int32),
        "row_s": pltpu.SMEM((NEIGH, BLOCKS), jnp.int32),
        "valid_s": pltpu.SMEM((NEIGH, BLOCKS), jnp.int32),
        "store": VM((16, NB_LEN, 128), BF16),
        "sums": VM((2, 8, WIDTH), F32),
        "out_sem": dma((CHUNKS,)),
        "fs": dma,
        "fr": dma,
    }
    for send, recv, shape in (
        ("ring_s", "ring_r", (2, 7, 2)),
        ("near_ss", "near_rs", (2,)),
        ("far_s", "far_r", (2,)),
        ("wring_s", "wring_r", (2, 8)),
        ("cell_s", "cell_r", (PLANE, 9)),
        ("wc_s", "wc_r", (PLANE, 9)),
        ("tab_ss", "tab_rs", (PLANE,)),
        ("ys_s", "ys_r", (2, CHUNKS)),
        ("yf_s", "yf_r", (2, CHUNKS)),
        ("cs", "cr", (2,)),
        ("xs", "xr", (2, NX - 1)),
        ("zs", "zr", (2, NZ - 1)),
    ):
        scratch[send] = dma(shape)
        scratch[recv] = dma(shape)
    anywhere = pl.BlockSpec(memory_space=pl.ANY)
    return pl.pallas_call(
        functools.partial(step_kernel, tuple(scratch)),
        out_shape=(
            jax.ShapeDtypeStruct((BLOCKS * BLOCK_LEN, WIDTH), BF16),
            jax.ShapeDtypeStruct((2, 8, WIDTH), F32),
        ),
        in_specs=[anywhere] * 8,
        out_specs=(anywhere, anywhere),
        scratch_shapes=[VM((16, NB_LEN, 128), BF16)] * 14 + list(scratch.values()),
        compiler_params=pltpu.CompilerParams(
            collective_id=0, has_side_effects=True, vmem_limit_bytes=VLIMIT
        ),
    )(store, key_weight, value_weight, owner.T, row.T, valid.T, queries, out_grad)


def finish_kernel(attended_in, sums_in, attended, key_out, value_out, held, sums, key, value, sem_in, sem_out, sem):
    count = sem_in.shape[0]
    size = held.shape[0] // count
    pieces = [pl.ds(i * size, size) for i in range(count)]
    first = pltpu.make_async_copy(sums_in, sums, sem.at[0])
    first.start()
    inward = [
        pltpu.make_async_copy(attended_in.at[piece], held.at[piece], sem_in.at[i])
        for i, piece in enumerate(pieces)
    ]
    outward = [
        pltpu.make_async_copy(held.at[piece], attended.at[piece], sem_out.at[i])
        for i, piece in enumerate(pieces)
    ]
    outward += [
        pltpu.make_async_copy(key, key_out, sem.at[1]),
        pltpu.make_async_copy(value, value_out, sem.at[2]),
    ]
    for copy in inward:
        copy.start()
    low = lax.axis_index("dp") % 2 == 0
    first.wait()
    key[...] = jnp.where(low, sums[0, :4], sums[0, 4:])
    value[...] = jnp.where(low, sums[1, :4], sums[1, 4:])
    for copy in outward[count:]:
        copy.start()
    for i in range(count):
        inward[i].wait()
        outward[i].start()
    for copy in outward:
        copy.wait()


def finish(attended, sums):
    anywhere = pl.BlockSpec(memory_space=pl.ANY)
    dma = pltpu.SemaphoreType.DMA
    gradient = (4, WIDTH)
    return pl.pallas_call(
        finish_kernel,
        out_shape=(
            jax.ShapeDtypeStruct(attended.shape, BF16),
            jax.ShapeDtypeStruct(gradient, F32),
            jax.ShapeDtypeStruct(gradient, F32),
        ),
        in_specs=[anywhere] * 2,
        out_specs=(anywhere,) * 3,
        scratch_shapes=[
            VM(attended.shape, BF16),
            VM(sums.shape, F32),
            VM(gradient, F32),
            VM(gradient, F32),
            dma((CHUNKS,)),
            dma((CHUNKS,)),
            dma((3,)),
        ],
        compiler_params=pltpu.CompilerParams(vmem_limit_bytes=VLIMIT),
    )(attended, sums)


def shards(queries, out_grad, store, key_weight, value_weight, owner, row, valid):
    attended, sums = step(
        queries, out_grad, store, key_weight, value_weight, owner, row, valid
    )
    return finish(attended, sums)


def solution(mesh):
    in_specs = (
        P("dp", "mp"),
        P("dp", "mp"),
        P("dp", None, "mp"),
        P("dp", "mp"),
        P("dp", "mp"),
        P("dp", None),
        P("dp", None),
        P("dp", None),
    )
    out_specs = (P("dp", "mp"), P("dp", "mp"), P("dp", "mp"))
    return jax.shard_map(shards, mesh=mesh, in_specs=in_specs, out_specs=out_specs, check_vma=False)
```
